256 devices in a mesh: outer: 8 (over y, x_hi), fsdp: 8 (over z), tp: 4 (over x_lo, core).
Axes of the slice: x: 4 (x_hi: 2, x_lo: 2; x = x_hi * 2 + x_lo), y: 4, z: 8, core: 2. Of those that a mesh axis runs over, the one named last changes fastest.
Arguments:
- pseudo_grad: float32 [8, 512, 12288], P('outer', 'fsdp', 'tp'), may hold values from -6 to 6
- outer_params: float32 [512, 12288], P('fsdp', 'tp'), may hold values from -6 to 6
- momentum: float32 [512, 12288], P('fsdp', 'tp'), may hold values from -6 to 6
- hidden: bfloat16 [8, 3072, 12288], P('outer', 'fsdp', 'tp'), may hold values from -6 to 6
- kv_weight: bfloat16 [8, 12288, 1024], P('outer', 'fsdp', 'tp'), may hold values from -0.0546875 to 0.0546875
- kv_cotangent: bfloat16 [8, 3072, 1024], P('outer', 'fsdp', 'tp'), may hold values from -4 to 4
Outputs:
- new_params: float32 [512, 12288], P('fsdp', 'tp')
- new_momentum: float32 [512, 12288], P('fsdp', 'tp')
- keys_values: bfloat16 [8, 3072, 1024], P('outer', 'fsdp', 'tp')
- input_grad: bfloat16 [8, 3072, 12288], P('outer', 'fsdp', 'tp')
- weight_grad: bfloat16 [8, 12288, 1024], P('outer', 'fsdp', 'tp')
The draws below stay inside these ranges and needn't reach their ends.
All inputs are finite; a program needn't handle non-finite values.
Results may differ from the reference program's by a relative error of at most 0.017.
Values may be sent and summed in bfloat16 or wider, within the bound.
A program may use at most 128 MiB of HBM per device.

```python
import jax
import jax.numpy as jnp
from jax import lax

D = 12288
KVW = 512
TOK_DEV = 384
TOKENS = 3072
SLAB = 512
N_OUTER = 8
N_FSDP = 8
N_TP = 4


def spiked(array, key, source, target, parts, factor):
    def block_of(axis_at):
        return (jnp.arange(array.shape[axis_at]) // (array.shape[axis_at] // parts)).reshape((-1,) + (1,) * (array.ndim - 1 - axis_at))

    one_side = jax.random.permutation(key, parts)[block_of(target)]
    far = (block_of(target) + parts // 2) % parts
    return jnp.where((block_of(source) == one_side) | (block_of(source) == far), factor * array, array)


def block_levels(key, extent, split, smallest, high):
    factor_of = 1.0
    for position, blocks in split:
        steps = jax.random.uniform(jax.random.fold_in(jax.random.fold_in(key, 6), position), (blocks,), jnp.float32, smallest / len(split), high / len(split))
        factor_of = factor_of * jnp.repeat(jnp.exp(steps), extent[position] // blocks).reshape((-1,) + (1,) * (len(extent) - 1 - position))
    return factor_of


def gaussian(stream_key, dims, deviation, bound, cuts=(), held_as=jnp.bfloat16):
    gain = block_levels(stream_key, dims, cuts, -0.22, 0.18) if cuts else 1.0
    values = jax.random.normal(stream_key, dims, jnp.float32) * deviation * gain
    return jnp.minimum(jnp.maximum(values, -bound), bound).astype(held_as)


def noise_with(rng, dims, deviation, most, shards, heavy, kind=jnp.bfloat16):
    entries = deviation * jax.random.normal(rng, dims, jnp.float32)
    if shards:
        entries = entries * block_levels(rng, dims, shards, -0.22, 0.18)
    return jnp.clip(spiked(entries, jax.random.fold_in(rng, 3), *heavy), -most, most).astype(kind)


def setup_inputs(seed: int = 0) -> dict:
    seeds = jax.random.split(jax.random.key(seed), 7)
    return {
        "pseudo_grad": gaussian(seeds[0], (N_OUTER, SLAB, D), 1.0, 6.0, ((0, 8), (1, 8), (2, 4)), jnp.float32),
        "outer_params": gaussian(seeds[1], (SLAB, D), 1.0, 6.0, ((0, 8), (1, 4)), jnp.float32),
        "momentum": gaussian(seeds[2], (SLAB, D), 1.0, 6.0, ((0, 8), (1, 4)), jnp.float32),
        "hidden": noise_with(seeds[3], (N_OUTER, TOKENS, D), 1.0, 6.0, ((0, 8), (1, 8), (2, 4)), (1, 2, 8, 2.0)),
        "kv_weight": gaussian(seeds[4], (N_OUTER, D, 2 * KVW), D ** -0.5, 0.0546875, ((0, 8), (1, 8), (2, 4))),
        "kv_cotangent": gaussian(seeds[5], (N_OUTER, TOKENS, 2 * KVW), 0.25, 4.0, ((0, 8), (1, 8), (2, 4))),
    }


outer_beta = 0.9
outer_rate = 0.7


def pod_inner(operands):
    tokens, weights, cotangent = operands
    keys_values = jnp.dot(tokens, weights, preferred_element_type=jnp.float32).astype(jnp.bfloat16)
    group_width = cotangent.shape[1] // N_TP
    input_sum = jnp.zeros((tokens.shape[0], tokens.shape[1]), jnp.float32)
    for group in range(N_TP):
        cot_group = cotangent[:, group * group_width:(group + 1) * group_width]
        weight_group = weights[:, group * group_width:(group + 1) * group_width]
        part = lax.dot_general(cot_group, weight_group, (((1,), (1,)), ((), ())), preferred_element_type=jnp.float32)
        part_rounded = lax.optimization_barrier(part.astype(jnp.bfloat16))
        input_sum = input_sum + part_rounded.astype(jnp.float32)
    input_grad = input_sum.astype(jnp.bfloat16)
    token_blocks = tokens.reshape(N_FSDP, TOK_DEV, tokens.shape[1])
    cot_blocks = cotangent.reshape(N_FSDP, TOK_DEV, cotangent.shape[1])

    def add_block(running, block):
        block_tokens, block_cot = block
        term = lax.dot_general(block_tokens, block_cot, (((0,), (0,)), ((), ())), preferred_element_type=jnp.float32)
        rounded = lax.optimization_barrier(term.astype(jnp.bfloat16))
        return running + rounded.astype(jnp.float32), None

    start_sum = jnp.zeros((tokens.shape[1], cotangent.shape[1]), jnp.float32)
    summed, _ = lax.scan(add_block, start_sum, (token_blocks, cot_blocks))
    return keys_values, input_grad, summed.astype(jnp.bfloat16)


def reference(pseudo_grad, outer_params, momentum, hidden, kv_weight, kv_cotangent):
    average = jnp.sum(pseudo_grad, axis=0) / N_OUTER
    new_momentum = outer_beta * momentum + average
    new_params = outer_params - outer_rate * (average + outer_beta * new_momentum)
    keys_values, input_grad, weight_grad = lax.map(pod_inner, (hidden, kv_weight, kv_cotangent))
    return new_params, new_momentum, keys_values, input_grad, weight_grad
```

```python
import functools

import jax
import jax.numpy as jnp
from jax import lax
from jax.experimental import pallas as pl
from jax.experimental.pallas import tpu as pltpu
from jax.sharding import PartitionSpec as P

outer_beta = 0.9
outer_rate = 0.7
MESH = pl.DeviceIdType.MESH
BF = jnp.bfloat16
F32 = jnp.float32

Z = 8
PIECES = 16
STEPS = 7


def nesterov(average, params_old, moment_old):
    moment_new = outer_beta * moment_old + average
    params_new = params_old - outer_rate * (average + outer_beta * moment_new)
    return (params_new, moment_new)


def kernel(
    hid_in, w_in, cot_in,
    kv_out, ig_out, wg_out,
    hid, wfull, cot, cot_t, part, sib, far, rs_out, rs_in, kv_acc, kv_stage, ig_stage, wg_stage,
    load_sem, store_sem,
    ag_send, ag_recv, rs_send, rs_recv,
    hx_send, hx_recv, hs_send, hs_recv, hf_send, hf_recv,
    p_send, p_recv, s_send, s_recv,
):
    z = lax.axis_index("fsdp")
    t = lax.axis_index("tp")
    x = t // 2
    c = lax.rem(t, 2)
    sibling = 2 * x + (1 - c)
    peer = 2 * (1 - x) + c
    up = lax.rem(z + 1, Z)
    down = lax.rem(z + Z - 1, Z)
    half = w_in.shape[0] // 2

    def remote(src, dst, send, recv, where):
        return pltpu.make_async_remote_copy(
            src_ref=src, dst_ref=dst, send_sem=send, recv_sem=recv, device_id=where, device_id_type=MESH
        )

    barrier = pltpu.get_barrier_semaphore()
    for where in ({"fsdp": up}, {"fsdp": down}, {"tp": sibling}, {"tp": peer}):
        pl.semaphore_signal(barrier, inc=1, device_id=where, device_id_type=MESH)
    pl.semaphore_wait(barrier, 4)

    def ring(block):
        return lax.rem(block + 2 * Z, Z)

    def ag_piece(j, direction, at):
        if direction == 0:
            return 2 * ring(at - j // 2) + lax.rem(j, 2)
        return 2 * ring(at + j // 2) + 1 - lax.rem(j, 2)

    def ag_copy(j, direction):
        b = ag_piece(j, direction, z)
        return remote(
            wfull.at[b], wfull.at[b], ag_send.at[direction, j], ag_recv.at[direction, j],
            {"fsdp": up if direction == 0 else down},
        )

    def ag_first(j, direction):
        h = j if direction == 0 else 1 - j
        return remote(
            w_in.at[pl.ds(h * half, half)], wfull.at[2 * z + h], ag_send.at[direction, j], ag_recv.at[direction, j],
            {"fsdp": up if direction == 0 else down},
        )

    for j in range(2):
        for direction in range(2):
            ag_first(j, direction).start()

    def hid_view(k):
        return hid_in.at[:, pl.ds(k * half, half)]

    def hx_copy(k):
        return remote(hid_view(k), hid.at[4 * t + k], hx_send.at[k], hx_recv.at[k], {"tp": peer})

    def hs_copy(k):
        return remote(hid_view(k), hid.at[4 * t + k], hs_send.at[k], hs_recv.at[k], {"tp": sibling})

    def hf_copy(k):
        return remote(hid.at[4 * peer + k], hid.at[4 * peer + k], hf_send.at[k], hf_recv.at[k], {"tp": sibling})

    for k in range(4):
        hx_copy(k).start()
    loads = [pltpu.make_async_copy(cot_in, cot, load_sem.at[0])]
    for h in range(2):
        loads.append(pltpu.make_async_copy(w_in.at[pl.ds(h * half, half)], wfull.at[2 * z + h], load_sem.at[1 + h]))
    for k in range(4):
        loads.append(pltpu.make_async_copy(hid_view(k), hid.at[4 * t + k], load_sem.at[3 + k]))
    for copy in loads:
        copy.start()
    for k in range(4):
        hs_copy(k).start()
    for copy in loads:
        copy.wait()
    cot_t[...] = cot[...].astype(F32).T.astype(BF)

    def column_part(b):
        part[b] = lax.dot_general(
            cot[...], wfull[b], (((1,), (1,)), ((), ())), preferred_element_type=F32
        ).astype(BF)

    def slot_of(b):
        return 4 * (b // 8) + lax.rem(b, 4)

    def owner_core(b):
        return lax.rem(b // 4, 2)

    def p_copy(b):
        s = slot_of(b)
        return remote(part.at[b], sib.at[s], p_send.at[s], p_recv.at[s], {"tp": sibling})

    def s_copy(b):
        k = lax.rem(b, 4)
        return remote(part.at[b], far.at[k], s_send.at[k], s_recv.at[k], {"tp": peer})

    def make_part(b):
        column_part(b)

        @pl.when(owner_core(b) != c)
        def _():
            p_copy(b).start()

    def pair_part(b):
        @pl.when((owner_core(b) == c) & (b // 8 != x))
        def _():
            p_copy(b).wait_recv()
            part[b] = (part[b].astype(F32) + sib[slot_of(b)].astype(F32)).astype(BF)
            s_copy(b).start()

    make_part(2 * z)
    make_part(2 * z + 1)
    pair_part(2 * z)
    pair_part(2 * z + 1)

    def ag_step(j, carry):
        for direction in range(2):
            ag_copy(j, direction).wait_recv()

            @pl.when(j + 2 < STEPS)
            def _():
                ag_copy(j + 2, direction).start()

        here_up = ag_piece(j, 0, z - 1)
        here_down = ag_piece(j, 1, z + 1)
        make_part(here_up)
        make_part(here_down)
        for at, k in ((1, 0), (3, 1), (4, 2), (6, 3)):
            @pl.when(j == at)
            def _():
                hx_copy(k).wait_recv()
                hf_copy(k).start()
        pair_part(here_up)
        pair_part(here_down)
        return carry

    lax.fori_loop(0, STEPS, ag_step, 0)

    for k in range(4):
        hs_copy(k).wait_recv()
        hf_copy(k).wait_recv()

    def rs_piece(j, direction):
        if direction == 0:
            return 2 * ring(z + 4 - (j + 1) // 2) + lax.rem(j, 2)
        return 2 * ring(z - 4 + (j + 1) // 2) + 1 - lax.rem(j, 2)

    def rs_copy(j, direction):
        return remote(
            rs_out.at[direction, j], rs_in.at[direction, j], rs_send.at[direction, j], rs_recv.at[direction, j],
            {"fsdp": up if direction == 0 else down},
        )

    def token_sum(b):
        return jnp.dot(cot_t[...], hid[b], preferred_element_type=F32)

    for j in range(2):
        for direction in range(2):
            rs_out[direction, j] = token_sum(rs_piece(j, direction)).astype(BF)
            rs_copy(j, direction).start()

    kv_acc[...] = jnp.zeros_like(kv_acc)

    def rs_step(j, carry):
        for direction in range(2):
            mine = token_sum(rs_piece(j, direction))
            rs_copy(j - 2, direction).wait_recv()
            rs_out[direction, j] = (mine + rs_in[direction, j - 2].astype(F32)).astype(BF)
            rs_copy(j, direction).start()
        for i in range(3):
            b = 3 * (j - 2) + i
            kv_acc[...] += jnp.dot(hid[b], wfull[b], preferred_element_type=F32)
        return carry

    lax.fori_loop(2, STEPS, rs_step, 0)
    kv_stage[...] = (kv_acc[...] + jnp.dot(hid[15], wfull[15], preferred_element_type=F32)).astype(BF)
    stores = [pltpu.make_async_copy(kv_stage, kv_out, store_sem.at[0])]
    stores[0].start()

    for k in range(4):
        b = 4 * t + k
        p_copy(b).wait_recv()
        s_copy(b).wait_recv()
        total = part[b].astype(F32) + sib[4 * x + k].astype(F32) + far[k].astype(F32)
        ig_stage[k] = total.astype(BF)
        stores.append(pltpu.make_async_copy(ig_stage.at[k], ig_out.at[:, pl.ds(k * half, half)], store_sem.at[1 + k]))
        stores[-1].start()

    for direction in range(2):
        rs_copy(5, direction).wait_recv()
    for direction in range(2):
        rs_copy(6, direction).wait_recv()
    for h in range(2):
        total = token_sum(2 * z + h) + rs_in[0, 6 - h].astype(F32) + rs_in[1, 5 + h].astype(F32)
        wg_stage[pl.ds(h * half, half)] = total.T.astype(BF)
        stores.append(
            pltpu.make_async_copy(
                wg_stage.at[pl.ds(h * half, half)], wg_out.at[pl.ds(h * half, half)], store_sem.at[5 + h]
            )
        )
        stores[-1].start()

    for j in range(STEPS):
        for direction in range(2):
            ag_copy(j, direction).wait_send()
            rs_copy(j, direction).wait_send()
    for k in range(4):
        hx_copy(k).wait_send()
        hs_copy(k).wait_send()
        hf_copy(k).wait_send()
        s_copy(4 * peer + k).wait_send()
        p_copy(4 * sibling + k).wait_send()
        p_copy(4 * (3 - t) + k).wait_send()
    for copy in stores:
        copy.wait()


def inner(hidden, weights, cotangent):
    tokens, width = hidden.shape
    rows, cols = weights.shape
    half = rows // 2
    sems = pltpu.SemaphoreType.DMA
    any_spec = pl.BlockSpec(memory_space=pl.ANY)
    return pl.pallas_call(
        kernel,
        out_shape=(
            jax.ShapeDtypeStruct((tokens, cols), BF),
            jax.ShapeDtypeStruct((tokens, width), BF),
            jax.ShapeDtypeStruct((rows, cols), BF),
        ),
        in_specs=[any_spec] * 3,
        out_specs=[any_spec] * 3,
        scratch_shapes=[
            pltpu.VMEM((PIECES, tokens, half), BF),
            pltpu.VMEM((PIECES, half, cols), BF),
            pltpu.VMEM((tokens, cols), BF),
            pltpu.VMEM((cols, tokens), BF),
            pltpu.VMEM((PIECES, tokens, half), BF),
            pltpu.VMEM((8, tokens, half), BF),
            pltpu.VMEM((4, tokens, half), BF),
            pltpu.VMEM((2, STEPS, cols, half), BF),
            pltpu.VMEM((2, STEPS, cols, half), BF),
            pltpu.VMEM((tokens, cols), F32),
            pltpu.VMEM((tokens, cols), BF),
            pltpu.VMEM((4, tokens, half), BF),
            pltpu.VMEM((rows, cols), BF),
            sems((7,)), sems((7,)),
            sems((2, STEPS)), sems((2, STEPS)), sems((2, STEPS)), sems((2, STEPS)),
            sems((4,)), sems((4,)), sems((4,)), sems((4,)), sems((4,)), sems((4,)),
            sems((8,)), sems((8,)), sems((4,)), sems((4,)),
        ],
        compiler_params=pltpu.CompilerParams(
            collective_id=0, has_side_effects=True, vmem_limit_bytes=60 * 1024 * 1024
        ),
        cost_estimate=pl.CostEstimate(flops=7_250_000_000, bytes_accessed=8_000_000, transcendentals=0),
        name="inner_step",
    )(hidden, weights, cotangent)


def per_device(pseudo_grad, outer_params, momentum, hidden, kv_weight, kv_cotangent):
    keys_values, input_grad, weight_grad = inner(hidden[0], kv_weight[0], kv_cotangent[0])
    pods = lax.axis_size("outer")
    average = lax.psum(pseudo_grad[0].astype(BF), "outer").astype(F32) / pods
    new_params, new_momentum = nesterov(average, outer_params, momentum)
    return (new_params, new_momentum, keys_values[None], input_grad[None], weight_grad[None])


def solution(mesh):
    return jax.shard_map(
        per_device,
        mesh=mesh,
        in_specs=(
            P("outer", "fsdp", "tp"),
            P("fsdp", "tp"),
            P("fsdp", "tp"),
            P("outer", "fsdp", "tp"),
            P("outer", "fsdp", "tp"),
            P("outer", "fsdp", "tp"),
        ),
        out_specs=(
            P("fsdp", "tp"),
            P("fsdp", "tp"),
            P("outer", "fsdp", "tp"),
            P("outer", "fsdp", "tp"),
            P("outer", "fsdp", "tp"),
        ),
        check_vma=False,
    )
```

```python
import jax
import jax.numpy as jnp
from jax import lax
from jax.experimental import pallas as pl
from jax.experimental.pallas import tpu as pltpu
from jax.sharding import PartitionSpec as P

outer_beta = 0.9
outer_rate = 0.7
MESH = pl.DeviceIdType.MESH
BF = jnp.bfloat16
F32 = jnp.float32

Z = 8
Y = 4
PIECES = 16
STEPS = 7


def nesterov(average, params_old, moment_old):
    moment_new = outer_beta * moment_old + average
    params_new = params_old - outer_rate * (average + outer_beta * moment_new)
    return (params_new, moment_new)


def kernel(
    pg_in, par_in, mom_in, hid_in, w_in, cot_in,
    par_out, mom_out, kv_out, ig_out, wg_out,
    hid, wfull, cot, cot_t, part, sib, far, rs_out, rs_in, kv_acc, kv_stage, ig_stage, wg_stage,
    pg, par, mom, y_out, y_in, pod_out, pod_in, avg,
    load_sem, store_sem,
    ag_send, ag_recv, rs_send, rs_recv,
    hx_send, hx_recv, hs_send, hs_recv,
    p_send, p_recv, s_send, s_recv,
    y_send, y_recv, v_send, v_recv, pod_send, pod_recv,
):
    o = lax.axis_index("outer")
    z = lax.axis_index("fsdp")
    t = lax.axis_index("tp")
    x = t // 2
    c = lax.rem(t, 2)
    sibling = 2 * x + (1 - c)
    peer = 2 * (1 - x) + c
    diagonal = 3 - t
    up = lax.rem(z + 1, Z)
    down = lax.rem(z + Z - 1, Z)
    y = o // 2
    x_hi = lax.rem(o, 2)
    other_hi = 2 * y + 1 - x_hi
    y_at = [lax.rem(y + i, Y) for i in range(Y)]
    half = w_in.shape[0] // 2
    quarter = pg_in.shape[1] // Y

    def remote(src, dst, send, recv, where):
        return pltpu.make_async_remote_copy(
            src_ref=src, dst_ref=dst, send_sem=send, recv_sem=recv, device_id=where, device_id_type=MESH
        )

    barrier = pltpu.get_barrier_semaphore()
    partners = [{"fsdp": up}, {"fsdp": down}, {"tp": sibling}, {"tp": peer}, {"outer": other_hi}]
    partners += [{"outer": 2 * y_at[i] + x_hi} for i in range(1, Y)]
    for where in partners:
        pl.semaphore_signal(barrier, inc=1, device_id=where, device_id_type=MESH)
    pl.semaphore_wait(barrier, len(partners))

    def ring(block):
        return lax.rem(block + 2 * Z, Z)

    def ag_piece(j, direction, at):
        if direction == 0:
            return 2 * ring(at - j // 2) + lax.rem(j, 2)
        return 2 * ring(at + j // 2) + 1 - lax.rem(j, 2)

    def ag_copy(j, direction):
        b = ag_piece(j, direction, z)
        return remote(
            wfull.at[b], wfull.at[b], ag_send.at[direction, j], ag_recv.at[direction, j],
            {"fsdp": up if direction == 0 else down},
        )

    def ag_first(j, direction):
        h = j if direction == 0 else 1 - j
        return remote(
            w_in.at[pl.ds(h * half, half)], wfull.at[2 * z + h], ag_send.at[direction, j], ag_recv.at[direction, j],
            {"fsdp": up if direction == 0 else down},
        )

    for j in range(2):
        for direction in range(2):
            ag_first(j, direction).start()

    def farther(of):
        low = ring(2 * of - z)
        high = ring(2 * of + 1 - z)
        return (jnp.minimum(high, Z - high) > jnp.minimum(low, Z - low)).astype(jnp.int32)

    def hid_turn(i, of):
        first = farther(of)
        return 2 * lax.rem(first + i // 2, 2) + i % 2

    def hid_view(k):
        return hid_in.at[:, pl.ds(pl.multiple_of(k * half, half), half)]

    def hx_copy(i):
        k = hid_turn(i, t)
        return remote(hid_view(k), hid.at[4 * t + k], hx_send.at[i], hx_recv.at[i], {"tp": peer})

    def hs_copy(k):
        b = 4 * t + k
        return remote(hid_view(k), hid.at[b], hs_send.at[k], hs_recv.at[b], {"tp": sibling})

    def hf_copy(i):
        b = 4 * peer + hid_turn(i, peer)
        return remote(hid.at[b], hid.at[b], hs_send.at[4 + i], hs_recv.at[b], {"tp": sibling})

    for i in range(4):
        hx_copy(i).start()
    loads = [pltpu.make_async_copy(cot_in, cot, load_sem.at[0])]
    for h in range(2):
        loads.append(pltpu.make_async_copy(w_in.at[pl.ds(h * half, half)], wfull.at[2 * z + h], load_sem.at[1 + h]))
    for k in range(4):
        loads.append(pltpu.make_async_copy(hid_view(k), hid.at[4 * t + k], load_sem.at[3 + k]))
    loads.append(pltpu.make_async_copy(pg_in, pg, load_sem.at[7]))
    loads.append(pltpu.make_async_copy(par_in, par, load_sem.at[8]))
    loads.append(pltpu.make_async_copy(mom_in, mom, load_sem.at[9]))
    for copy in loads:
        copy.start()
    for k in range(4):
        hs_copy(k).start()
    for copy in loads:
        copy.wait()
    cot_t[...] = cot[...].astype(F32).T.astype(BF)

    def y_copy(i):
        return remote(y_out.at[i], y_in.at[i], y_send.at[i], y_recv.at[i], {"outer": 2 * y_at[i] + x_hi})

    def pod_copy():
        return remote(pod_out, pod_in, pod_send, pod_recv, {"outer": other_hi})

    def v_copy(i):
        return remote(avg.at[y], avg.at[y], v_send.at[i], v_recv.at[i], {"outer": 2 * y_at[i] + x_hi})

    def pg_quarter(at):
        return pg[:, pl.ds(pl.multiple_of(at * quarter, quarter), quarter)].astype(BF)

    for i in range(1, Y):
        y_out[i] = pg_quarter(y_at[i])
        y_copy(i).start()

    def column_part(b):
        part[b] = lax.dot_general(
            cot[...], wfull[b], (((1,), (1,)), ((), ())), preferred_element_type=F32
        ).astype(BF)

    def slot_of(b):
        return 4 * (b // 8) + lax.rem(b, 4)

    def owner_core(b):
        return lax.rem(b // 4, 2)

    def p_copy(b):
        s = slot_of(b)
        return remote(part.at[b], sib.at[s], p_send.at[s], p_recv.at[s], {"tp": sibling})

    def s_copy(b):
        k = lax.rem(b, 4)
        return remote(part.at[b], far.at[k], s_send.at[k], s_recv.at[k], {"tp": peer})

    def make_part(b):
        column_part(b)

        @pl.when(owner_core(b) != c)
        def _():
            p_copy(b).start()

    def pair_part(b):
        @pl.when((owner_core(b) == c) & (b // 8 != x))
        def _():
            p_copy(b).wait_recv()
            part[b] = (part[b].astype(F32) + sib[slot_of(b)].astype(F32)).astype(BF)
            s_copy(b).start()

    def pair_step(j, carry):
        pair_part(ag_piece(j, 0, z - 1))
        pair_part(ag_piece(j, 1, z + 1))
        return carry

    def rs_piece(j, direction):
        if direction == 0:
            return 2 * ring(z + 4 - (j + 1) // 2) + lax.rem(j, 2)
        return 2 * ring(z - 4 + (j + 1) // 2) + 1 - lax.rem(j, 2)

    def rs_copy(j, direction):
        return remote(
            rs_out.at[direction, j], rs_in.at[direction, j], rs_send.at[direction, j], rs_recv.at[direction, j],
            {"fsdp": up if direction == 0 else down},
        )

    def token_sum(b):
        @pl.when(owner_core(b) != c)
        def _():
            remote(hid.at[b], hid.at[b], hs_send.at[0], hs_recv.at[b], {"tp": sibling}).wait_recv()

        return jnp.dot(cot_t[...], hid[b], preferred_element_type=F32)

    def rs_start(j):
        for direction in range(2):
            rs_out[direction, j] = token_sum(rs_piece(j, direction)).astype(BF)
            rs_copy(j, direction).start()

    make_part(2 * z)
    make_part(2 * z + 1)

    def ag_step(j, carry):
        for direction in range(2):
            ag_copy(j, direction).wait_recv()

            @pl.when(j + 2 < STEPS)
            def _():
                ag_copy(j + 2, direction).start()

        make_part(ag_piece(j, 0, z - 1))
        make_part(ag_piece(j, 1, z + 1))
        for at, i in ((1, 0), (3, 1), (4, 2), (6, 3)):
            @pl.when(j == at)
            def _():
                hx_copy(i).wait_recv()
                hf_copy(i).start()

        @pl.when(j == 1)
        def _():
            total = pg_quarter(y).astype(F32)
            for i in range(1, Y):
                y_copy(i).wait_recv()
                total += y_in[i].astype(F32)
            pod_out[...] = total.astype(BF)
            pod_copy().start()

        @pl.when(j == 4)
        def _():
            pair_part(2 * z)
            pair_part(2 * z + 1)
            lax.fori_loop(0, 4, pair_step, 0)

        @pl.when(j == 5)
        def _():
            rs_start(0)

        @pl.when(j > 4)
        def _():
            pair_step(j - 1, 0)

        return carry

    lax.fori_loop(0, STEPS, ag_step, 0)
    rs_start(1)
    pair_step(STEPS - 1, 0)

    pod_copy().wait_recv()
    avg[y] = ((pod_out[...].astype(F32) + pod_in[...].astype(F32)) / (2 * Y)).astype(BF)
    for i in range(1, Y):
        v_copy(i).start()

    def add_keys_values(j):
        for direction in range(2):
            b = rs_piece(j, direction)
            kv_acc[...] += jnp.dot(hid[b], wfull[b], preferred_element_type=F32)

    kv_acc[...] = jnp.zeros_like(kv_acc)

    def rs_step(j, carry):
        for direction in range(2):
            mine = token_sum(rs_piece(j, direction))
            rs_copy(j - 2, direction).wait_recv()
            rs_out[direction, j] = (mine + rs_in[direction, j - 2].astype(F32)).astype(BF)
            rs_copy(j, direction).start()
        add_keys_values(j)
        return carry

    lax.fori_loop(2, STEPS, rs_step, 0)
    own = [token_sum(2 * z + h) for h in range(2)]
    for j in range(2):
        add_keys_values(j)
    for h in range(2):
        kv_acc[...] += jnp.dot(hid[2 * z + h], wfull[2 * z + h], preferred_element_type=F32)
    kv_stage[...] = kv_acc[...].astype(BF)
    stores = [pltpu.make_async_copy(kv_stage, kv_out, store_sem.at[0])]
    stores[0].start()

    for i in range(1, Y):
        v_copy(i).wait_recv()
    for i in range(Y):
        columns = pl.ds(i * quarter, quarter)
        average = avg[i].astype(F32)
        new_params, new_momentum = nesterov(average, par[:, columns], mom[:, columns])
        par[:, columns] = new_params
        mom[:, columns] = new_momentum
    stores.append(pltpu.make_async_copy(par, par_out, store_sem.at[7]))
    stores.append(pltpu.make_async_copy(mom, mom_out, store_sem.at[8]))
    stores[1].start()
    stores[2].start()

    for k in range(4):
        b = 4 * t + k
        p_copy(b).wait_recv()
        s_copy(b).wait_recv()
        total = part[b].astype(F32) + sib[4 * x + k].astype(F32) + far[k].astype(F32)
        ig_stage[k] = total.astype(BF)
        stores.append(pltpu.make_async_copy(ig_stage.at[k], ig_out.at[:, pl.ds(k * half, half)], store_sem.at[1 + k]))
        stores[-1].start()

    for direction in range(2):
        rs_copy(5, direction).wait_recv()
    for direction in range(2):
        rs_copy(6, direction).wait_recv()
    for h in range(2):
        total = own[h] + rs_in[0, 6 - h].astype(F32) + rs_in[1, 5 + h].astype(F32)
        wg_stage[pl.ds(h * half, half)] = total.T.astype(BF)
        stores.append(
            pltpu.make_async_copy(
                wg_stage.at[pl.ds(h * half, half)], wg_out.at[pl.ds(h * half, half)], store_sem.at[5 + h]
            )
        )
        stores[-1].start()

    for j in range(STEPS):
        for direction in range(2):
            ag_copy(j, direction).wait_send()
            rs_copy(j, direction).wait_send()
    for k in range(4):
        hx_copy(k).wait_send()
        hs_copy(k).wait_send()
        hf_copy(k).wait_send()
        s_copy(4 * peer + k).wait_send()
        p_copy(4 * sibling + k).wait_send()
        p_copy(4 * diagonal + k).wait_send()
    for i in range(1, Y):
        y_copy(i).wait_send()
        v_copy(i).wait_send()
    pod_copy().wait_send()
    for copy in stores:
        copy.wait()


def whole_step(pseudo_grad, params, momentum, hidden, weights, cotangent):
    tokens, width = hidden.shape
    rows, cols = weights.shape
    slab = params.shape
    half = rows // 2
    quarter = (slab[0], slab[1] // Y)
    sems = pltpu.SemaphoreType.DMA
    any_spec = pl.BlockSpec(memory_space=pl.ANY)
    return pl.pallas_call(
        kernel,
        out_shape=(
            jax.ShapeDtypeStruct(slab, F32),
            jax.ShapeDtypeStruct(slab, F32),
            jax.ShapeDtypeStruct((tokens, cols), BF),
            jax.ShapeDtypeStruct((tokens, width), BF),
            jax.ShapeDtypeStruct((rows, cols), BF),
        ),
        in_specs=[any_spec] * 6,
        out_specs=[any_spec] * 5,
        scratch_shapes=[
            pltpu.VMEM((PIECES, tokens, half), BF),
            pltpu.VMEM((PIECES, half, cols), BF),
            pltpu.VMEM((tokens, cols), BF),
            pltpu.VMEM((cols, tokens), BF),
            pltpu.VMEM((PIECES, tokens, half), BF),
            pltpu.VMEM((8, tokens, half), BF),
            pltpu.VMEM((4, tokens, half), BF),
            pltpu.VMEM((2, STEPS, cols, half), BF),
            pltpu.VMEM((2, STEPS, cols, half), BF),
            pltpu.VMEM((tokens, cols), F32),
            pltpu.VMEM((tokens, cols), BF),
            pltpu.VMEM((4, tokens, half), BF),
            pltpu.VMEM((rows, cols), BF),
            pltpu.VMEM(slab, F32),
            pltpu.VMEM(slab, F32),
            pltpu.VMEM(slab, F32),
            pltpu.VMEM((Y,) + quarter, BF),
            pltpu.VMEM((Y,) + quarter, BF),
            pltpu.VMEM(quarter, BF),
            pltpu.VMEM(quarter, BF),
            pltpu.VMEM((Y,) + quarter, BF),
            sems((10,)), sems((9,)),
            sems((2, STEPS)), sems((2, STEPS)), sems((2, STEPS)), sems((2, STEPS)),
            sems((4,)), sems((4,)), sems((8,)), sems((PIECES,)),
            sems((8,)), sems((8,)), sems((4,)), sems((4,)),
            sems((Y,)), sems((Y,)), sems((Y,)), sems((Y,)), sems, sems,
        ],
        compiler_params=pltpu.CompilerParams(
            collective_id=0, has_side_effects=True, vmem_limit_bytes=60 * 1024 * 1024
        ),
        cost_estimate=pl.CostEstimate(flops=7_250_000_000, bytes_accessed=12_000_000, transcendentals=0),
        name="whole_step",
    )(pseudo_grad, params, momentum, hidden, weights, cotangent)


def per_device(pseudo_grad, outer_params, momentum, hidden, kv_weight, kv_cotangent):
    new_params, new_momentum, keys_values, input_grad, weight_grad = whole_step(
        pseudo_grad[0], outer_params, momentum, hidden[0], kv_weight[0], kv_cotangent[0]
    )
    return (new_params, new_momentum, keys_values[None], input_grad[None], weight_grad[None])


def solution(mesh):
    return jax.shard_map(
        per_device,
        mesh=mesh,
        in_specs=(
            P("outer", "fsdp", "tp"),
            P("fsdp", "tp"),
            P("fsdp", "tp"),
            P("outer", "fsdp", "tp"),
            P("outer", "fsdp", "tp"),
            P("outer", "fsdp", "tp"),
        ),
        out_specs=(
            P("fsdp", "tp"),
            P("fsdp", "tp"),
            P("outer", "fsdp", "tp"),
            P("outer", "fsdp", "tp"),
            P("outer", "fsdp", "tp"),
        ),
        check_vma=False,
    )
```

```python
import jax
import jax.numpy as jnp
from jax import lax
from jax.experimental import pallas as pl
from jax.experimental.pallas import tpu as pltpu
from jax.sharding import PartitionSpec as P

outer_beta = 0.9
outer_rate = 0.7
MESH = pl.DeviceIdType.MESH
BF = jnp.bfloat16
F32 = jnp.float32

Z = 8
Y = 4
PIECES = 16
STEPS = 7


def nesterov(average, params_old, moment_old):
    moment_new = outer_beta * moment_old + average
    params_new = params_old - outer_rate * (average + outer_beta * moment_new)
    return (params_new, moment_new)


def kernel(
    pg_in, par_in, mom_in, hid_in, w_in, cot_in,
    par_out, mom_out, kv_out, ig_out, wg_out,
    hid, wfull, cot, cot_t, part, sib, far, rs_out, rs_in, kv_acc,
    pg, par, mom, y_out, y_in, pod_out, pod_in, avg,
    load_sem,
    ag_send, ag_recv, rs_send, rs_recv,
    hx_send, hx_recv, hs_send, hs_recv,
    p_send, p_recv, s_send, s_recv,
    y_send, y_recv, v_send, v_recv, pod_send, pod_recv,
):
    o = lax.axis_index("outer")
    z = lax.axis_index("fsdp")
    t = lax.axis_index("tp")
    x = t // 2
    c = lax.rem(t, 2)
    sibling = 2 * x + (1 - c)
    peer = 2 * (1 - x) + c
    diagonal = 3 - t
    up = lax.rem(z + 1, Z)
    down = lax.rem(z + Z - 1, Z)
    y = o // 2
    x_hi = lax.rem(o, 2)
    other_hi = 2 * y + 1 - x_hi
    y_at = [lax.rem(y + i, Y) for i in range(Y)]
    half = w_in.shape[0] // 2
    quarter = pg_in.shape[1] // Y

    def remote(src, dst, send, recv, where):
        return pltpu.make_async_remote_copy(
            src_ref=src, dst_ref=dst, send_sem=send, recv_sem=recv, device_id=where, device_id_type=MESH
        )

    barrier = pltpu.get_barrier_semaphore()
    partners = [{"fsdp": up}, {"fsdp": down}, {"tp": sibling}, {"tp": peer}, {"outer": other_hi}]
    partners += [{"outer": 2 * y_at[i] + x_hi} for i in range(1, Y)]
    for where in partners:
        pl.semaphore_signal(barrier, inc=1, device_id=where, device_id_type=MESH)
    pl.semaphore_wait(barrier, len(partners))

    def ring(block):
        return lax.rem(block + 2 * Z, Z)

    def ag_piece(j, direction, at):
        if direction == 0:
            return 2 * ring(at - j // 2) + lax.rem(j, 2)
        return 2 * ring(at + j // 2) + 1 - lax.rem(j, 2)

    def ag_copy(j, direction):
        b = ag_piece(j, direction, z)
        return remote(
            wfull.at[b], wfull.at[b], ag_send.at[direction, j], ag_recv.at[direction, j],
            {"fsdp": up if direction == 0 else down},
        )

    def ag_first(j, direction):
        h = j if direction == 0 else 1 - j
        return remote(
            w_in.at[pl.ds(h * half, half)], wfull.at[2 * z + h], ag_send.at[direction, j], ag_recv.at[direction, j],
            {"fsdp": up if direction == 0 else down},
        )

    for j in range(2):
        for direction in range(2):
            ag_first(j, direction).start()

    def farther(of):
        low = ring(2 * of - z)
        high = ring(2 * of + 1 - z)
        return (jnp.minimum(high, Z - high) > jnp.minimum(low, Z - low)).astype(jnp.int32)

    def hid_turn(i, of):
        first = farther(of)
        return 2 * lax.rem(first + i // 2, 2) + i % 2

    def hid_view(k):
        return hid_in.at[:, pl.ds(pl.multiple_of(k * half, half), half)]

    def hx_copy(i):
        k = hid_turn(i, t)
        return remote(hid_view(k), hid.at[4 * t + k], hx_send.at[i], hx_recv.at[i], {"tp": peer})

    def hs_copy(k):
        b = 4 * t + k
        return remote(hid_view(k), hid.at[b], hs_send.at[k], hs_recv.at[b], {"tp": sibling})

    def hf_copy(i):
        b = 4 * peer + hid_turn(i, peer)
        return remote(hid.at[b], hid.at[b], hs_send.at[4 + i], hs_recv.at[b], {"tp": sibling})

    for i in range(4):
        hx_copy(i).start()
    loads = [pltpu.make_async_copy(cot_in, cot, load_sem.at[0])]
    for h in range(2):
        loads.append(pltpu.make_async_copy(w_in.at[pl.ds(h * half, half)], wfull.at[2 * z + h], load_sem.at[1 + h]))
    for k in range(4):
        loads.append(pltpu.make_async_copy(hid_view(k), hid.at[4 * t + k], load_sem.at[3 + k]))
    loads.append(pltpu.make_async_copy(pg_in, pg, load_sem.at[7]))
    loads.append(pltpu.make_async_copy(par_in, par, load_sem.at[8]))
    loads.append(pltpu.make_async_copy(mom_in, mom, load_sem.at[9]))
    for copy in loads:
        copy.start()
    for k in range(4):
        hs_copy(k).start()
    for copy in loads:
        copy.wait()
    cot_t[...] = cot[...].astype(F32).T.astype(BF)

    def y_copy(i):
        return remote(y_out.at[i], y_in.at[i], y_send.at[i], y_recv.at[i], {"outer": 2 * y_at[i] + x_hi})

    def pod_copy():
        return remote(pod_out, pod_in, pod_send, pod_recv, {"outer": other_hi})

    def v_copy(i):
        return remote(avg.at[y], avg.at[y], v_send.at[i], v_recv.at[i], {"outer": 2 * y_at[i] + x_hi})

    def pg_quarter(at):
        return pg[:, pl.ds(pl.multiple_of(at * quarter, quarter), quarter)].astype(BF)

    for i in range(1, Y):
        y_out[i] = pg_quarter(y_at[i])
        y_copy(i).start()

    def column_part(b):
        part[b] = lax.dot_general(
            cot[...], wfull[b], (((1,), (1,)), ((), ())), preferred_element_type=F32
        ).astype(BF)

    def slot_of(b):
        return 4 * (b // 8) + lax.rem(b, 4)

    def owner_core(b):
        return lax.rem(b // 4, 2)

    def p_copy(b):
        s = slot_of(b)
        return remote(part.at[b], sib.at[s], p_send.at[s], p_recv.at[s], {"tp": sibling})

    def s_copy(b):
        k = lax.rem(b, 4)
        return remote(part.at[b], far.at[k], s_send.at[k], s_recv.at[k], {"tp": peer})

    def make_part(b):
        column_part(b)

        @pl.when(owner_core(b) != c)
        def _():
            p_copy(b).start()

    def pair_part(b):
        @pl.when((owner_core(b) == c) & (b // 8 != x))
        def _():
            p_copy(b).wait_recv()
            part[b] = (part[b].astype(F32) + sib[slot_of(b)].astype(F32)).astype(BF)
            s_copy(b).start()

    def pair_step(j, carry):
        pair_part(ag_piece(j, 0, z - 1))
        pair_part(ag_piece(j, 1, z + 1))
        return carry

    def rs_piece(j, direction):
        if direction == 0:
            return 2 * ring(z + 4 - (j + 1) // 2) + lax.rem(j, 2)
        return 2 * ring(z - 4 + (j + 1) // 2) + 1 - lax.rem(j, 2)

    def rs_copy(j, direction):
        return remote(
            rs_out.at[direction, j], rs_in.at[direction, j], rs_send.at[direction, j], rs_recv.at[direction, j],
            {"fsdp": up if direction == 0 else down},
        )

    def token_sum(b):
        @pl.when(owner_core(b) != c)
        def _():
            remote(hid.at[b], hid.at[b], hs_send.at[0], hs_recv.at[b], {"tp": sibling}).wait_recv()

        return jnp.dot(cot_t[...], hid[b], preferred_element_type=F32)

    def rs_start(j):
        for direction in range(2):
            rs_out[direction, j] = token_sum(rs_piece(j, direction)).astype(BF)
            rs_copy(j, direction).start()

    make_part(2 * z)
    make_part(2 * z + 1)

    def ag_step(j, carry):
        for direction in range(2):
            ag_copy(j, direction).wait_recv()

            @pl.when(j + 2 < STEPS)
            def _():
                ag_copy(j + 2, direction).start()

        make_part(ag_piece(j, 0, z - 1))
        make_part(ag_piece(j, 1, z + 1))
        for at, i in ((1, 0), (3, 1), (4, 2), (6, 3)):
            @pl.when(j == at)
            def _():
                hx_copy(i).wait_recv()
                hf_copy(i).start()

        @pl.when(j == 1)
        def _():
            total = pg_quarter(y).astype(F32)
            for i in range(1, Y):
                y_copy(i).wait_recv()
                total += y_in[i].astype(F32)
            pod_out[...] = total.astype(BF)
            pod_copy().start()

        @pl.when(j == 4)
        def _():
            pair_part(2 * z)
            pair_part(2 * z + 1)
            lax.fori_loop(0, 4, pair_step, 0)

        @pl.when(j == 5)
        def _():
            rs_start(0)

        @pl.when(j > 4)
        def _():
            pair_step(j - 1, 0)

        return carry

    lax.fori_loop(0, STEPS, ag_step, 0)
    rs_start(1)
    pair_step(STEPS - 1, 0)

    pod_copy().wait_recv()
    avg[y] = ((pod_out[...].astype(F32) + pod_in[...].astype(F32)) / (2 * Y)).astype(BF)
    for i in range(1, Y):
        v_copy(i).start()

    def add_keys_values(j):
        for direction in range(2):
            b = rs_piece(j, direction)
            kv_acc[...] += jnp.dot(hid[b], wfull[b], preferred_element_type=F32)

    kv_acc[...] = jnp.zeros_like(kv_acc)

    def rs_step(j, carry):
        for direction in range(2):
            mine = token_sum(rs_piece(j, direction))
            rs_copy(j - 2, direction).wait_recv()
            rs_out[direction, j] = (mine + rs_in[direction, j - 2].astype(F32)).astype(BF)
            rs_copy(j, direction).start()
        add_keys_values(j)
        return carry

    lax.fori_loop(2, STEPS, rs_step, 0)
    own = [token_sum(2 * z + h) for h in range(2)]
    for j in range(2):
        add_keys_values(j)
    for h in range(2):
        kv_acc[...] += jnp.dot(hid[2 * z + h], wfull[2 * z + h], preferred_element_type=F32)
    kv_out[...] = kv_acc[...].astype(BF)

    for i in range(1, Y):
        v_copy(i).wait_recv()
    for i in range(Y):
        columns = pl.ds(i * quarter, quarter)
        average = avg[i].astype(F32)
        new_params, new_momentum = nesterov(average, par[:, columns], mom[:, columns])
        par_out[:, columns] = new_params
        mom_out[:, columns] = new_momentum

    for k in range(4):
        b = 4 * t + k
        p_copy(b).wait_recv()
        s_copy(b).wait_recv()
        total = part[b].astype(F32) + sib[4 * x + k].astype(F32) + far[k].astype(F32)
        ig_out[:, pl.ds(k * half, half)] = total.astype(BF)

    for direction in range(2):
        rs_copy(5, direction).wait_recv()
    for direction in range(2):
        rs_copy(6, direction).wait_recv()
    for h in range(2):
        total = own[h] + rs_in[0, 6 - h].astype(F32) + rs_in[1, 5 + h].astype(F32)
        wg_out[pl.ds(h * half, half)] = total.T.astype(BF)

    for j in range(STEPS):
        for direction in range(2):
            ag_copy(j, direction).wait_send()
            rs_copy(j, direction).wait_send()
    for k in range(4):
        hx_copy(k).wait_send()
        hs_copy(k).wait_send()
        hf_copy(k).wait_send()
        s_copy(4 * peer + k).wait_send()
        p_copy(4 * sibling + k).wait_send()
        p_copy(4 * diagonal + k).wait_send()
    for i in range(1, Y):
        y_copy(i).wait_send()
        v_copy(i).wait_send()
    pod_copy().wait_send()


def whole_step(pseudo_grad, params, momentum, hidden, weights, cotangent):
    tokens, width = hidden.shape
    rows, cols = weights.shape
    slab = params.shape
    half = rows // 2
    quarter = (slab[0], slab[1] // Y)
    sems = pltpu.SemaphoreType.DMA
    any_spec = pl.BlockSpec(memory_space=pl.ANY)
    return pl.pallas_call(
        kernel,
        out_shape=(
            pltpu.VMEM(slab, F32),
            pltpu.VMEM(slab, F32),
            pltpu.VMEM((tokens, cols), BF),
            pltpu.VMEM((tokens, width), BF),
            pltpu.VMEM((rows, cols), BF),
        ),
        in_specs=[any_spec] * 6,
        out_specs=[pl.BlockSpec(memory_space=pltpu.VMEM)] * 5,
        scratch_shapes=[
            pltpu.VMEM((PIECES, tokens, half), BF),
            pltpu.VMEM((PIECES, half, cols), BF),
            pltpu.VMEM((tokens, cols), BF),
            pltpu.VMEM((cols, tokens), BF),
            pltpu.VMEM((PIECES, tokens, half), BF),
            pltpu.VMEM((8, tokens, half), BF),
            pltpu.VMEM((4, tokens, half), BF),
            pltpu.VMEM((2, STEPS, cols, half), BF),
            pltpu.VMEM((2, STEPS, cols, half), BF),
            pltpu.VMEM((tokens, cols), F32),
            pltpu.VMEM(slab, F32),
            pltpu.VMEM(slab, F32),
            pltpu.VMEM(slab, F32),
            pltpu.VMEM((Y,) + quarter, BF),
            pltpu.VMEM((Y,) + quarter, BF),
            pltpu.VMEM(quarter, BF),
            pltpu.VMEM(quarter, BF),
            pltpu.VMEM((Y,) + quarter, BF),
            sems((10,)),
            sems((2, STEPS)), sems((2, STEPS)), sems((2, STEPS)), sems((2, STEPS)),
            sems((4,)), sems((4,)), sems((8,)), sems((PIECES,)),
            sems((8,)), sems((8,)), sems((4,)), sems((4,)),
            sems((Y,)), sems((Y,)), sems((Y,)), sems((Y,)), sems, sems,
        ],
        compiler_params=pltpu.CompilerParams(
            collective_id=0, has_side_effects=True, vmem_limit_bytes=56 * 1024 * 1024
        ),
        cost_estimate=pl.CostEstimate(flops=7_250_000_000, bytes_accessed=12_000_000, transcendentals=0),
        name="whole_step",
    )(pseudo_grad, params, momentum, hidden, weights, cotangent)


def store_kernel(*refs):
    sems = refs[-1]
    count = (len(refs) - 1) // 2
    copies = [pltpu.make_async_copy(refs[i], refs[count + i], sems.at[i]) for i in range(count)]
    for copy in copies:
        copy.start()
    for copy in copies:
        copy.wait()


def store(*results):
    any_spec = pl.BlockSpec(memory_space=pl.ANY)
    return pl.pallas_call(
        store_kernel,
        out_shape=tuple(pltpu.HBM(r.shape, r.dtype) for r in results),
        in_specs=[pl.BlockSpec(memory_space=pltpu.VMEM)] * len(results),
        out_specs=[pl.BlockSpec(memory_space=pltpu.HBM)] * len(results),
        scratch_shapes=[pltpu.SemaphoreType.DMA((len(results),))],
        compiler_params=pltpu.CompilerParams(vmem_limit_bytes=1024 * 1024),
        name="store_results",
    )(*results)


def per_device(pseudo_grad, outer_params, momentum, hidden, kv_weight, kv_cotangent):
    new_params, new_momentum, keys_values, input_grad, weight_grad = store(
        *(
            pltpu.with_memory_space_constraint(r, pltpu.VMEM)
            for r in whole_step(pseudo_grad[0], outer_params, momentum, hidden[0], kv_weight[0], kv_cotangent[0])
        )
    )
    return (new_params, new_momentum, keys_values[None], input_grad[None], weight_grad[None])


def solution(mesh):
    return jax.shard_map(
        per_device,
        mesh=mesh,
        in_specs=(
            P("outer", "fsdp", "tp"),
            P("fsdp", "tp"),
            P("fsdp", "tp"),
            P("outer", "fsdp", "tp"),
            P("outer", "fsdp", "tp"),
            P("outer", "fsdp", "tp"),
        ),
        out_specs=(
            P("fsdp", "tp"),
            P("fsdp", "tp"),
            P("outer", "fsdp", "tp"),
            P("outer", "fsdp", "tp"),
            P("outer", "fsdp", "tp"),
        ),
        check_vma=False,
    )
```

```python
import jax
import jax.numpy as jnp
from jax import lax
from jax.experimental import pallas as pl
from jax.experimental.pallas import tpu as pltpu
from jax.sharding import PartitionSpec as P

outer_beta = 0.9
outer_rate = 0.7
MESH = pl.DeviceIdType.MESH
BF = jnp.bfloat16
F32 = jnp.float32

Z = 8
Y = 4
PIECES = 16
STEPS = 7


def nesterov(average, params_old, moment_old):
    moment_new = outer_beta * moment_old + average
    params_new = params_old - outer_rate * (average + outer_beta * moment_new)
    return (params_new, moment_new)


def kernel(
    pg_in, par_in, mom_in, hid_in, w_in, cot_in,
    par_out, mom_out, kv_out, ig_out, wg_out,
    hid, wfull, cot, cot_t, part, sib, far, rs_out, rs_in, rs_own, kv_acc,
    pg, par, mom, y_out, y_in, pod_out, pod_in, avg,
    load_sem,
    ag_send, ag_recv, rs_send, rs_recv,
    hx_send, hx_recv, hs_send, hs_recv,
    p_send, p_recv, s_send, s_recv,
    y_send, y_recv, v_send, v_recv, pod_send, pod_recv,
):
    o = lax.axis_index("outer")
    z = lax.axis_index("fsdp")
    t = lax.axis_index("tp")
    x = t // 2
    c = lax.rem(t, 2)
    sibling = 2 * x + (1 - c)
    peer = 2 * (1 - x) + c
    diagonal = 3 - t
    up = lax.rem(z + 1, Z)
    down = lax.rem(z + Z - 1, Z)
    y = o // 2
    x_hi = lax.rem(o, 2)
    other_hi = 2 * y + 1 - x_hi
    y_at = [lax.rem(y + i, Y) for i in range(Y)]
    half = w_in.shape[0] // 2
    quarter = pg_in.shape[1] // Y

    def remote(src, dst, send, recv, where):
        return pltpu.make_async_remote_copy(
            src_ref=src, dst_ref=dst, send_sem=send, recv_sem=recv, device_id=where, device_id_type=MESH
        )

    barrier = pltpu.get_barrier_semaphore()
    partners = [{"fsdp": up}, {"fsdp": down}, {"tp": sibling}, {"tp": peer}, {"outer": other_hi}]
    partners += [{"outer": 2 * y_at[i] + x_hi} for i in range(1, Y)]
    for where in partners:
        pl.semaphore_signal(barrier, inc=1, device_id=where, device_id_type=MESH)
    pl.semaphore_wait(barrier, len(partners))

    def ring(block):
        return lax.rem(block + 2 * Z, Z)

    def ag_piece(j, direction, at):
        if direction == 0:
            return 2 * ring(at - j // 2) + lax.rem(j, 2)
        return 2 * ring(at + j // 2) + 1 - lax.rem(j, 2)

    def ag_copy(j, direction):
        b = ag_piece(j, direction, z)
        return remote(
            wfull.at[b], wfull.at[b], ag_send.at[direction, j], ag_recv.at[direction, j],
            {"fsdp": up if direction == 0 else down},
        )

    def ag_first(j, direction):
        h = j if direction == 0 else 1 - j
        return remote(
            w_in.at[pl.ds(h * half, half)], wfull.at[2 * z + h], ag_send.at[direction, j], ag_recv.at[direction, j],
            {"fsdp": up if direction == 0 else down},
        )

    for j in range(2):
        for direction in range(2):
            ag_first(j, direction).start()

    def farther(of):
        low = ring(2 * of - z)
        high = ring(2 * of + 1 - z)
        return (jnp.minimum(high, Z - high) > jnp.minimum(low, Z - low)).astype(jnp.int32)

    def hid_turn(i, of):
        first = farther(of)
        return 2 * lax.rem(first + i // 2, 2) + i % 2

    def hid_view(k):
        return hid_in.at[:, pl.ds(pl.multiple_of(k * half, half), half)]

    def hx_copy(i):
        k = hid_turn(i, t)
        return remote(hid_view(k), hid.at[4 * t + k], hx_send.at[i], hx_recv.at[i], {"tp": peer})

    def hs_copy(k):
        b = 4 * t + k
        return remote(hid_view(k), hid.at[b], hs_send.at[k], hs_recv.at[b], {"tp": sibling})

    def hf_copy(i):
        b = 4 * peer + hid_turn(i, peer)
        return remote(hid.at[b], hid.at[b], hs_send.at[4 + i], hs_recv.at[b], {"tp": sibling})

    for i in range(4):
        hx_copy(i).start()
    loads = [pltpu.make_async_copy(cot_in, cot, load_sem.at[0])]
    for h in range(2):
        loads.append(pltpu.make_async_copy(w_in.at[pl.ds(h * half, half)], wfull.at[2 * z + h], load_sem.at[1 + h]))
    for k in range(4):
        loads.append(pltpu.make_async_copy(hid_view(k), hid.at[4 * t + k], load_sem.at[3 + k]))
    loads.append(pltpu.make_async_copy(pg_in, pg, load_sem.at[7]))
    loads.append(pltpu.make_async_copy(par_in, par, load_sem.at[8]))
    loads.append(pltpu.make_async_copy(mom_in, mom, load_sem.at[9]))
    for copy in loads:
        copy.start()
    for k in range(4):
        hs_copy(k).start()
    for copy in loads:
        copy.wait()
    cot_t[...] = cot[...].astype(F32).T.astype(BF)

    def y_copy(i):
        return remote(y_out.at[i], y_in.at[i], y_send.at[i], y_recv.at[i], {"outer": 2 * y_at[i] + x_hi})

    def pod_copy():
        return remote(pod_out, pod_in, pod_send, pod_recv, {"outer": other_hi})

    def v_copy(i):
        return remote(avg.at[y], avg.at[y], v_send.at[i], v_recv.at[i], {"outer": 2 * y_at[i] + x_hi})

    def pg_quarter(at):
        return pg[:, pl.ds(pl.multiple_of(at * quarter, quarter), quarter)].astype(BF)

    for i in range(1, Y):
        y_out[i] = pg_quarter(y_at[i])
        y_copy(i).start()

    def column_part(b):
        part[b] = lax.dot_general(
            cot[...], wfull[b], (((1,), (1,)), ((), ())), preferred_element_type=F32
        ).astype(BF)

    def slot_of(b):
        return 4 * (b // 8) + lax.rem(b, 4)

    def owner_core(b):
        return lax.rem(b // 4, 2)

    def p_copy(b):
        s = slot_of(b)
        return remote(part.at[b], sib.at[s], p_send.at[s], p_recv.at[s], {"tp": sibling})

    def s_copy(b):
        k = lax.rem(b, 4)
        return remote(part.at[b], far.at[k], s_send.at[k], s_recv.at[k], {"tp": peer})

    def make_part(b):
        column_part(b)

        @pl.when(owner_core(b) != c)
        def _():
            p_copy(b).start()

    def pair_part(b):
        @pl.when((owner_core(b) == c) & (b // 8 != x))
        def _():
            p_copy(b).wait_recv()
            part[b] = (part[b].astype(F32) + sib[slot_of(b)].astype(F32)).astype(BF)
            s_copy(b).start()

    def pair_step(j, carry):
        pair_part(ag_piece(j, 0, z - 1))
        pair_part(ag_piece(j, 1, z + 1))
        return carry

    def rs_piece(j, direction):
        if direction == 0:
            return 2 * ring(z + 4 - (j + 1) // 2) + lax.rem(j, 2)
        return 2 * ring(z - 4 + (j + 1) // 2) + 1 - lax.rem(j, 2)

    def rs_copy(j, direction):
        return remote(
            rs_out.at[direction, j], rs_in.at[direction, j], rs_send.at[direction, j], rs_recv.at[direction, j],
            {"fsdp": up if direction == 0 else down},
        )

    def token_sum(b):
        @pl.when(owner_core(b) != c)
        def _():
            remote(hid.at[b], hid.at[b], hs_send.at[0], hs_recv.at[b], {"tp": sibling}).wait_recv()

        return jnp.dot(cot_t[...], hid[b], preferred_element_type=F32).T

    def rs_start(j):
        for direction in range(2):
            rs_out[direction, j] = token_sum(rs_piece(j, direction)).astype(BF)
            rs_copy(j, direction).start()

    make_part(2 * z)
    make_part(2 * z + 1)

    def ag_step(j, carry):
        for direction in range(2):
            ag_copy(j, direction).wait_recv()

            @pl.when(j + 2 < STEPS)
            def _():
                ag_copy(j + 2, direction).start()

        make_part(ag_piece(j, 0, z - 1))
        make_part(ag_piece(j, 1, z + 1))
        for at, i in ((1, 0), (3, 1), (4, 2), (6, 3)):
            @pl.when(j == at)
            def _():
                hx_copy(i).wait_recv()
                hf_copy(i).start()

        @pl.when(j == 1)
        def _():
            total = pg_quarter(y).astype(F32)
            for i in range(1, Y):
                y_copy(i).wait_recv()
                total += y_in[i].astype(F32)
            pod_out[...] = total.astype(BF)
            pod_copy().start()

        @pl.when(j == 4)
        def _():
            pair_part(2 * z)
            pair_part(2 * z + 1)
            lax.fori_loop(0, 4, pair_step, 0)

        @pl.when(j == 5)
        def _():
            rs_start(0)

        @pl.when(j > 4)
        def _():
            pair_step(j - 1, 0)

        return carry

    lax.fori_loop(0, STEPS, ag_step, 0)
    rs_start(1)
    pair_step(STEPS - 1, 0)

    pod_copy().wait_recv()
    avg[y] = ((pod_out[...].astype(F32) + pod_in[...].astype(F32)) / (2 * Y)).astype(BF)
    for i in range(1, Y):
        v_copy(i).start()

    def add_keys_values(j):
        for direction in range(2):
            b = rs_piece(j, direction)
            kv_acc[...] += jnp.dot(hid[b], wfull[b], preferred_element_type=F32)

    kv_acc[...] = jnp.zeros_like(kv_acc)

    def rs_step(j, carry):
        for direction in range(2):
            mine = token_sum(rs_piece(j, direction))
            rs_copy(j - 2, direction).wait_recv()
            rs_out[direction, j] = (mine + rs_in[direction, j - 2].astype(F32)).astype(BF)
            rs_copy(j, direction).start()
        add_keys_values(j)
        return carry

    lax.fori_loop(2, STEPS - 1, rs_step, 0)

    def last_copy(part_at, direction):
        rows = pl.ds(part_at * (half // 2), half // 2)
        return remote(
            rs_out.at[direction, STEPS - 1, rows], rs_in.at[direction, STEPS - 1, rows],
            rs_send.at[direction, STEPS - 1 + part_at], rs_recv.at[direction, STEPS - 1 + part_at],
            {"fsdp": up if direction == 0 else down},
        )

    mine = [token_sum(rs_piece(STEPS - 1, direction)) for direction in range(2)]
    for direction in range(2):
        rs_copy(STEPS - 3, direction).wait_recv()
        for part_at in range(2):
            low, high = part_at * (half // 2), (part_at + 1) * (half // 2)
            total = mine[direction][low:high] + rs_in[direction, STEPS - 3, low:high].astype(F32)
            rs_out[direction, STEPS - 1, low:high] = total.astype(BF)
            last_copy(part_at, direction).start()
    add_keys_values(STEPS - 1)
    for h in range(2):
        rs_own[h] = token_sum(2 * z + h)
    for j in range(2):
        add_keys_values(j)
    for h in range(2):
        kv_acc[...] += jnp.dot(hid[2 * z + h], wfull[2 * z + h], preferred_element_type=F32)
    kv_out[...] = kv_acc[...].astype(BF)

    for i in range(1, Y):
        v_copy(i).wait_recv()
    for i in range(Y):
        columns = pl.ds(i * quarter, quarter)
        average = avg[i].astype(F32)
        new_params, new_momentum = nesterov(average, par[:, columns], mom[:, columns])
        par_out[:, columns] = new_params
        mom_out[:, columns] = new_momentum

    for k in range(4):
        b = 4 * t + k
        p_copy(b).wait_recv()
        s_copy(b).wait_recv()
        total = part[b].astype(F32) + sib[4 * x + k].astype(F32) + far[k].astype(F32)
        ig_out[:, pl.ds(k * half, half)] = total.astype(BF)

    for j in range(STEPS):
        for direction in range(2):
            ag_copy(j, direction).wait_send()
            if j < STEPS - 2:
                rs_copy(j, direction).wait_send()
    for k in range(4):
        hx_copy(k).wait_send()
        hs_copy(k).wait_send()
        hf_copy(k).wait_send()
        s_copy(4 * peer + k).wait_send()
        p_copy(4 * sibling + k).wait_send()
        p_copy(4 * diagonal + k).wait_send()
    for i in range(1, Y):
        y_copy(i).wait_send()
        v_copy(i).wait_send()
    pod_copy().wait_send()

    for direction in range(2):
        rs_copy(STEPS - 2, direction).wait_recv()
        rs_own[1 - direction] += rs_in[direction, STEPS - 2].astype(F32)
    for part_at in range(2):
        for direction in range(2):
            last_copy(part_at, direction).wait_recv()
            low, high = part_at * (half // 2), (part_at + 1) * (half // 2)
            total = rs_own[direction, low:high] + rs_in[direction, STEPS - 1, low:high].astype(F32)
            wg_out[direction * half + low:direction * half + high] = total.astype(BF)
    for direction in range(2):
        rs_copy(STEPS - 2, direction).wait_send()
        for part_at in range(2):
            last_copy(part_at, direction).wait_send()


def whole_step(pseudo_grad, params, momentum, hidden, weights, cotangent):
    tokens, width = hidden.shape
    rows, cols = weights.shape
    slab = params.shape
    half = rows // 2
    quarter = (slab[0], slab[1] // Y)
    sems = pltpu.SemaphoreType.DMA
    any_spec = pl.BlockSpec(memory_space=pl.ANY)
    return pl.pallas_call(
        kernel,
        out_shape=(
            pltpu.VMEM(slab, F32),
            pltpu.VMEM(slab, F32),
            pltpu.VMEM((tokens, cols), BF),
            pltpu.VMEM((tokens, width), BF),
            pltpu.VMEM((rows, cols), BF),
        ),
        in_specs=[any_spec] * 6,
        out_specs=[pl.BlockSpec(memory_space=pltpu.VMEM)] * 5,
        scratch_shapes=[
            pltpu.VMEM((PIECES, tokens, half), BF),
            pltpu.VMEM((PIECES, half, cols), BF),
            pltpu.VMEM((tokens, cols), BF),
            pltpu.VMEM((cols, tokens), BF),
            pltpu.VMEM((PIECES, tokens, half), BF),
            pltpu.VMEM((8, tokens, half), BF),
            pltpu.VMEM((4, tokens, half), BF),
            pltpu.VMEM((2, STEPS, half, cols), BF),
            pltpu.VMEM((2, STEPS, half, cols), BF),
            pltpu.VMEM((2, half, cols), F32),
            pltpu.VMEM((tokens, cols), F32),
            pltpu.VMEM(slab, F32),
            pltpu.VMEM(slab, F32),
            pltpu.VMEM(slab, F32),
            pltpu.VMEM((Y,) + quarter, BF),
            pltpu.VMEM((Y,) + quarter, BF),
            pltpu.VMEM(quarter, BF),
            pltpu.VMEM(quarter, BF),
            pltpu.VMEM((Y,) + quarter, BF),
            sems((10,)),
            sems((2, STEPS)), sems((2, STEPS)), sems((2, STEPS + 1)), sems((2, STEPS + 1)),
            sems((4,)), sems((4,)), sems((8,)), sems((PIECES,)),
            sems((8,)), sems((8,)), sems((4,)), sems((4,)),
            sems((Y,)), sems((Y,)), sems((Y,)), sems((Y,)), sems, sems,
        ],
        compiler_params=pltpu.CompilerParams(
            collective_id=0, has_side_effects=True, vmem_limit_bytes=56 * 1024 * 1024
        ),
        cost_estimate=pl.CostEstimate(flops=7_250_000_000, bytes_accessed=12_000_000, transcendentals=0),
        name="whole_step",
    )(pseudo_grad, params, momentum, hidden, weights, cotangent)


def store_kernel(*refs):
    sems = refs[-1]
    count = (len(refs) - 1) // 2
    copies = [pltpu.make_async_copy(refs[i], refs[count + i], sems.at[i]) for i in range(count)]
    for copy in copies:
        copy.start()
    for copy in copies:
        copy.wait()


def store(*results):
    any_spec = pl.BlockSpec(memory_space=pl.ANY)
    return pl.pallas_call(
        store_kernel,
        out_shape=tuple(pltpu.HBM(r.shape, r.dtype) for r in results),
        in_specs=[pl.BlockSpec(memory_space=pltpu.VMEM)] * len(results),
        out_specs=[pl.BlockSpec(memory_space=pltpu.HBM)] * len(results),
        scratch_shapes=[pltpu.SemaphoreType.DMA((len(results),))],
        compiler_params=pltpu.CompilerParams(vmem_limit_bytes=1024 * 1024),
        name="store_results",
    )(*results)


def per_device(pseudo_grad, outer_params, momentum, hidden, kv_weight, kv_cotangent):
    new_params, new_momentum, keys_values, input_grad, weight_grad = store(
        *(
            pltpu.with_memory_space_constraint(r, pltpu.VMEM)
            for r in whole_step(pseudo_grad[0], outer_params, momentum, hidden[0], kv_weight[0], kv_cotangent[0])
        )
    )
    return (new_params, new_momentum, keys_values[None], input_grad[None], weight_grad[None])


def solution(mesh):
    return jax.shard_map(
        per_device,
        mesh=mesh,
        in_specs=(
            P("outer", "fsdp", "tp"),
            P("fsdp", "tp"),
            P("fsdp", "tp"),
            P("outer", "fsdp", "tp"),
            P("outer", "fsdp", "tp"),
            P("outer", "fsdp", "tp"),
        ),
        out_specs=(
            P("fsdp", "tp"),
            P("fsdp", "tp"),
            P("outer", "fsdp", "tp"),
            P("outer", "fsdp", "tp"),
            P("outer", "fsdp", "tp"),
        ),
        check_vma=False,
    )
```

```python
import jax
import jax.numpy as jnp
from jax import lax
from jax.experimental import pallas as pl
from jax.experimental.pallas import tpu as pltpu
from jax.sharding import PartitionSpec as P

outer_beta = 0.9
outer_rate = 0.7
MESH = pl.DeviceIdType.MESH
BF = jnp.bfloat16
F32 = jnp.float32

Z = 8
Y = 4
PIECES = 16
STEPS = 7


def nesterov(average, params_old, moment_old):
    moment_new = outer_beta * moment_old + average
    params_new = params_old - outer_rate * (average + outer_beta * moment_new)
    return (params_new, moment_new)


def kernel(
    pg_in, par_in, mom_in, hid_in, w_in, cot_in,
    par_out, mom_out, kv_out, ig_out, wg_out,
    hid, wfull, cot, cot_t, part, sib, far, rs_out, rs_in, rs_own, kv_acc,
    pg, par, mom, y_out, y_in, pod_out, pod_in, avg,
    load_sem,
    ag_send, ag_recv, rs_send, rs_recv,
    hx_send, hx_recv, hs_send, hs_recv,
    p_send, p_recv, s_send, s_recv,
    y_send, y_recv, v_send, v_recv, pod_send, pod_recv, here_sem,
):
    o = lax.axis_index("outer")
    z = lax.axis_index("fsdp")
    t = lax.axis_index("tp")
    x = t // 2
    c = lax.rem(t, 2)
    sibling = 2 * x + (1 - c)
    peer = 2 * (1 - x) + c
    diagonal = 3 - t
    up = lax.rem(z + 1, Z)
    down = lax.rem(z + Z - 1, Z)
    y = o // 2
    x_hi = lax.rem(o, 2)
    other_hi = 2 * y + 1 - x_hi
    y_at = [lax.rem(y + i, Y) for i in range(Y)]
    half = w_in.shape[0] // 2
    quarter = pg_in.shape[1] // Y

    def remote(src, dst, send, recv, where):
        return pltpu.make_async_remote_copy(
            src_ref=src, dst_ref=dst, send_sem=send, recv_sem=recv, device_id=where, device_id_type=MESH
        )

    barrier = pltpu.get_barrier_semaphore()
    partners = [{"fsdp": up}, {"fsdp": down}, {"tp": sibling}, {"tp": peer}]
    for where in partners:
        pl.semaphore_signal(barrier, inc=1, device_id=where, device_id_type=MESH)
    pods = [other_hi] + [2 * y_at[i] + x_hi for i in range(1, Y)]
    lower = 0
    for pod in pods:
        lower += (pod < o).astype(jnp.int32)

        @pl.when(pod > o)
        def _():
            pl.semaphore_signal(barrier, inc=1, device_id={"outer": pod}, device_id_type=MESH)

    pl.semaphore_wait(barrier, len(partners) + lower)

    def ring(block):
        return lax.rem(block + 2 * Z, Z)

    def ag_piece(j, direction, at):
        if direction == 0:
            return 2 * ring(at - j // 2) + lax.rem(j, 2)
        return 2 * ring(at + j // 2) + 1 - lax.rem(j, 2)

    def ag_copy(j, direction):
        b = ag_piece(j, direction, z)
        return remote(
            wfull.at[b], wfull.at[b], ag_send.at[direction, j], ag_recv.at[direction, j],
            {"fsdp": up if direction == 0 else down},
        )

    def ag_first(j, direction):
        h = j if direction == 0 else 1 - j
        return remote(
            w_in.at[pl.ds(h * half, half)], wfull.at[2 * z + h], ag_send.at[direction, j], ag_recv.at[direction, j],
            {"fsdp": up if direction == 0 else down},
        )

    for j in range(2):
        for direction in range(2):
            ag_first(j, direction).start()

    def farther(of):
        low = ring(2 * of - z)
        high = ring(2 * of + 1 - z)
        return (jnp.minimum(high, Z - high) > jnp.minimum(low, Z - low)).astype(jnp.int32)

    def hid_turn(i, of):
        first = farther(of)
        return 2 * lax.rem(first + i // 2, 2) + i % 2

    def hid_view(k):
        return hid_in.at[:, pl.ds(pl.multiple_of(k * half, half), half)]

    def hx_copy(i):
        k = hid_turn(i, t)
        return remote(hid_view(k), hid.at[4 * t + k], hx_send.at[i], hx_recv.at[i], {"tp": peer})

    def hs_copy(k):
        b = 4 * t + k
        return remote(hid_view(k), hid.at[b], hs_send.at[k], hs_recv.at[b], {"tp": sibling})

    def hf_copy(i):
        b = 4 * peer + hid_turn(i, peer)
        return remote(hid.at[b], hid.at[b], hs_send.at[4 + i], hs_recv.at[b], {"tp": sibling})

    for i in range(4):
        hx_copy(i).start()
    loads = [pltpu.make_async_copy(cot_in, cot, load_sem.at[0])]
    for h in range(2):
        loads.append(pltpu.make_async_copy(w_in.at[pl.ds(h * half, half)], wfull.at[2 * z + h], load_sem.at[1 + h]))
    for k in range(4):
        loads.append(pltpu.make_async_copy(hid_view(k), hid.at[4 * t + k], load_sem.at[3 + k]))
    loads.append(pltpu.make_async_copy(pg_in, pg, load_sem.at[7]))
    loads.append(pltpu.make_async_copy(par_in, par, load_sem.at[8]))
    loads.append(pltpu.make_async_copy(mom_in, mom, load_sem.at[9]))
    for copy in loads:
        copy.start()
    for k in range(4):
        hs_copy(k).start()
    for copy in loads:
        copy.wait()
    cot_t[...] = cot[...].astype(F32).T.astype(BF)

    def y_copy(i):
        return remote(y_out.at[i], y_in.at[i], y_send.at[i], y_recv.at[i], {"outer": 2 * y_at[i] + x_hi})

    def pod_copy():
        return remote(pod_out, pod_in, pod_send, pod_recv, {"outer": other_hi})

    def v_copy(i):
        return remote(avg.at[y], avg.at[y], v_send.at[i], v_recv.at[i], {"outer": 2 * y_at[i] + x_hi})

    def pg_quarter(at):
        return pg[:, pl.ds(pl.multiple_of(at * quarter, quarter), quarter)].astype(BF)

    for pod in pods:
        @pl.when(pod < o)
        def _():
            pl.semaphore_signal(here_sem, inc=1, device_id={"outer": pod}, device_id_type=MESH)

    def column_part(b):
        part[b] = lax.dot_general(
            cot[...], wfull[b], (((1,), (1,)), ((), ())), preferred_element_type=F32
        ).astype(BF)

    def slot_of(b):
        return 4 * (b // 8) + lax.rem(b, 4)

    def owner_core(b):
        return lax.rem(b // 4, 2)

    def p_copy(b):
        s = slot_of(b)
        return remote(part.at[b], sib.at[s], p_send.at[s], p_recv.at[s], {"tp": sibling})

    def s_copy(b):
        k = lax.rem(b, 4)
        return remote(part.at[b], far.at[k], s_send.at[k], s_recv.at[k], {"tp": peer})

    def make_part(b):
        column_part(b)

        @pl.when(owner_core(b) != c)
        def _():
            p_copy(b).start()

    def pair_part(b):
        @pl.when((owner_core(b) == c) & (b // 8 != x))
        def _():
            p_copy(b).wait_recv()
            part[b] = (part[b].astype(F32) + sib[slot_of(b)].astype(F32)).astype(BF)
            s_copy(b).start()

    def pair_step(j, carry):
        pair_part(ag_piece(j, 0, z - 1))
        pair_part(ag_piece(j, 1, z + 1))
        return carry

    def rs_piece(j, direction):
        if direction == 0:
            return 2 * ring(z + 4 - (j + 1) // 2) + lax.rem(j, 2)
        return 2 * ring(z - 4 + (j + 1) // 2) + 1 - lax.rem(j, 2)

    def rs_copy(j, direction):
        return remote(
            rs_out.at[direction, j], rs_in.at[direction, j], rs_send.at[direction, j], rs_recv.at[direction, j],
            {"fsdp": up if direction == 0 else down},
        )

    def token_sum(b):
        @pl.when(owner_core(b) != c)
        def _():
            remote(hid.at[b], hid.at[b], hs_send.at[0], hs_recv.at[b], {"tp": sibling}).wait_recv()

        return jnp.dot(cot_t[...], hid[b], preferred_element_type=F32).T

    def rs_start(j):
        for direction in range(2):
            rs_out[direction, j] = token_sum(rs_piece(j, direction)).astype(BF)
            rs_copy(j, direction).start()

    make_part(2 * z)
    make_part(2 * z + 1)

    def ag_step(j, carry):
        for direction in range(2):
            ag_copy(j, direction).wait_recv()

            @pl.when(j + 2 < STEPS)
            def _():
                ag_copy(j + 2, direction).start()

        make_part(ag_piece(j, 0, z - 1))
        make_part(ag_piece(j, 1, z + 1))
        for at, i in ((1, 0), (3, 1), (4, 2), (6, 3)):
            @pl.when(j == at)
            def _():
                hx_copy(i).wait_recv()
                hf_copy(i).start()

        @pl.when(j == 1)
        def _():
            @pl.when(lower < len(pods))
            def _():
                pl.semaphore_wait(here_sem, len(pods) - lower)

            for i in range(1, Y):
                y_out[i] = pg_quarter(y_at[i])
                y_copy(i).start()

        @pl.when(j == 3)
        def _():
            total = pg_quarter(y).astype(F32)
            for i in range(1, Y):
                y_copy(i).wait_recv()
                total += y_in[i].astype(F32)
            pod_out[...] = total.astype(BF)
            pod_copy().start()

        @pl.when(j == 4)
        def _():
            pair_part(2 * z)
            pair_part(2 * z + 1)
            lax.fori_loop(0, 4, pair_step, 0)

        @pl.when(j == 5)
        def _():
            rs_start(0)

        @pl.when(j > 4)
        def _():
            pair_step(j - 1, 0)

        return carry

    lax.fori_loop(0, STEPS, ag_step, 0)
    rs_start(1)
    pair_step(STEPS - 1, 0)

    pod_copy().wait_recv()
    avg[y] = ((pod_out[...].astype(F32) + pod_in[...].astype(F32)) / (2 * Y)).astype(BF)
    for i in range(1, Y):
        v_copy(i).start()

    def add_keys_values(j):
        for direction in range(2):
            b = rs_piece(j, direction)
            kv_acc[...] += jnp.dot(hid[b], wfull[b], preferred_element_type=F32)

    kv_acc[...] = jnp.zeros_like(kv_acc)

    def rs_step(j, carry):
        for direction in range(2):
            mine = token_sum(rs_piece(j, direction))
            rs_copy(j - 2, direction).wait_recv()
            rs_out[direction, j] = (mine + rs_in[direction, j - 2].astype(F32)).astype(BF)
            rs_copy(j, direction).start()
        add_keys_values(j)
        return carry

    lax.fori_loop(2, STEPS - 1, rs_step, 0)

    def last_copy(part_at, direction):
        rows = pl.ds(part_at * (half // 2), half // 2)
        return remote(
            rs_out.at[direction, STEPS - 1, rows], rs_in.at[direction, STEPS - 1, rows],
            rs_send.at[direction, STEPS - 1 + part_at], rs_recv.at[direction, STEPS - 1 + part_at],
            {"fsdp": up if direction == 0 else down},
        )

    mine = [token_sum(rs_piece(STEPS - 1, direction)) for direction in range(2)]
    for direction in range(2):
        rs_copy(STEPS - 3, direction).wait_recv()
        for part_at in range(2):
            low, high = part_at * (half // 2), (part_at + 1) * (half // 2)
            total = mine[direction][low:high] + rs_in[direction, STEPS - 3, low:high].astype(F32)
            rs_out[direction, STEPS - 1, low:high] = total.astype(BF)
            last_copy(part_at, direction).start()
    add_keys_values(STEPS - 1)
    for h in range(2):
        rs_own[h] = token_sum(2 * z + h)
    for j in range(2):
        add_keys_values(j)
    for h in range(2):
        kv_acc[...] += jnp.dot(hid[2 * z + h], wfull[2 * z + h], preferred_element_type=F32)
    kv_out[...] = kv_acc[...].astype(BF)

    for i in range(1, Y):
        v_copy(i).wait_recv()
    for i in range(Y):
        columns = pl.ds(i * quarter, quarter)
        average = avg[i].astype(F32)
        new_params, new_momentum = nesterov(average, par[:, columns], mom[:, columns])
        par_out[:, columns] = new_params
        mom_out[:, columns] = new_momentum

    for k in range(4):
        b = 4 * t + k
        p_copy(b).wait_recv()
        s_copy(b).wait_recv()
        total = part[b].astype(F32) + sib[4 * x + k].astype(F32) + far[k].astype(F32)
        ig_out[:, pl.ds(k * half, half)] = total.astype(BF)

    for j in range(STEPS):
        for direction in range(2):
            ag_copy(j, direction).wait_send()
            if j < STEPS - 2:
                rs_copy(j, direction).wait_send()
    for k in range(4):
        hx_copy(k).wait_send()
        hs_copy(k).wait_send()
        hf_copy(k).wait_send()
        s_copy(4 * peer + k).wait_send()
        p_copy(4 * sibling + k).wait_send()
        p_copy(4 * diagonal + k).wait_send()
    for i in range(1, Y):
        y_copy(i).wait_send()
        v_copy(i).wait_send()
    pod_copy().wait_send()

    for direction in range(2):
        rs_copy(STEPS - 2, direction).wait_recv()
        rs_own[1 - direction] += rs_in[direction, STEPS - 2].astype(F32)
    for part_at in range(2):
        for direction in range(2):
            last_copy(part_at, direction).wait_recv()
            low, high = part_at * (half // 2), (part_at + 1) * (half // 2)
            total = rs_own[direction, low:high] + rs_in[direction, STEPS - 1, low:high].astype(F32)
            wg_out[direction * half + low:direction * half + high] = total.astype(BF)
    for direction in range(2):
        rs_copy(STEPS - 2, direction).wait_send()
        for part_at in range(2):
            last_copy(part_at, direction).wait_send()


def whole_step(pseudo_grad, params, momentum, hidden, weights, cotangent):
    tokens, width = hidden.shape
    rows, cols = weights.shape
    slab = params.shape
    half = rows // 2
    quarter = (slab[0], slab[1] // Y)
    sems = pltpu.SemaphoreType.DMA
    any_spec = pl.BlockSpec(memory_space=pl.ANY)
    return pl.pallas_call(
        kernel,
        out_shape=(
            pltpu.VMEM(slab, F32),
            pltpu.VMEM(slab, F32),
            pltpu.VMEM((tokens, cols), BF),
            pltpu.VMEM((tokens, width), BF),
            pltpu.VMEM((rows, cols), BF),
        ),
        in_specs=[any_spec] * 6,
        out_specs=[pl.BlockSpec(memory_space=pltpu.VMEM)] * 5,
        scratch_shapes=[
            pltpu.VMEM((PIECES, tokens, half), BF),
            pltpu.VMEM((PIECES, half, cols), BF),
            pltpu.VMEM((tokens, cols), BF),
            pltpu.VMEM((cols, tokens), BF),
            pltpu.VMEM((PIECES, tokens, half), BF),
            pltpu.VMEM((8, tokens, half), BF),
            pltpu.VMEM((4, tokens, half), BF),
            pltpu.VMEM((2, STEPS, half, cols), BF),
            pltpu.VMEM((2, STEPS, half, cols), BF),
            pltpu.VMEM((2, half, cols), F32),
            pltpu.VMEM((tokens, cols), F32),
            pltpu.VMEM(slab, F32),
            pltpu.VMEM(slab, F32),
            pltpu.VMEM(slab, F32),
            pltpu.VMEM((Y,) + quarter, BF),
            pltpu.VMEM((Y,) + quarter, BF),
            pltpu.VMEM(quarter, BF),
            pltpu.VMEM(quarter, BF),
            pltpu.VMEM((Y,) + quarter, BF),
            sems((10,)),
            sems((2, STEPS)), sems((2, STEPS)), sems((2, STEPS + 1)), sems((2, STEPS + 1)),
            sems((4,)), sems((4,)), sems((8,)), sems((PIECES,)),
            sems((8,)), sems((8,)), sems((4,)), sems((4,)),
            sems((Y,)), sems((Y,)), sems((Y,)), sems((Y,)), sems, sems, pltpu.SemaphoreType.REGULAR,
        ],
        compiler_params=pltpu.CompilerParams(
            collective_id=0, has_side_effects=True, vmem_limit_bytes=56 * 1024 * 1024
        ),
        cost_estimate=pl.CostEstimate(flops=7_250_000_000, bytes_accessed=12_000_000, transcendentals=0),
        name="whole_step",
    )(pseudo_grad, params, momentum, hidden, weights, cotangent)


def store_kernel(*refs):
    sems = refs[-1]
    count = (len(refs) - 1) // 2
    copies = [pltpu.make_async_copy(refs[i], refs[count + i], sems.at[i]) for i in range(count)]
    for copy in copies:
        copy.start()
    for copy in copies:
        copy.wait()


def store(*results):
    any_spec = pl.BlockSpec(memory_space=pl.ANY)
    return pl.pallas_call(
        store_kernel,
        out_shape=tuple(pltpu.HBM(r.shape, r.dtype) for r in results),
        in_specs=[pl.BlockSpec(memory_space=pltpu.VMEM)] * len(results),
        out_specs=[pl.BlockSpec(memory_space=pltpu.HBM)] * len(results),
        scratch_shapes=[pltpu.SemaphoreType.DMA((len(results),))],
        compiler_params=pltpu.CompilerParams(vmem_limit_bytes=1024 * 1024),
        name="store_results",
    )(*results)


def per_device(pseudo_grad, outer_params, momentum, hidden, kv_weight, kv_cotangent):
    new_params, new_momentum, keys_values, input_grad, weight_grad = store(
        *(
            pltpu.with_memory_space_constraint(r, pltpu.VMEM)
            for r in whole_step(pseudo_grad[0], outer_params, momentum, hidden[0], kv_weight[0], kv_cotangent[0])
        )
    )
    return (new_params, new_momentum, keys_values[None], input_grad[None], weight_grad[None])


def solution(mesh):
    return jax.shard_map(
        per_device,
        mesh=mesh,
        in_specs=(
            P("outer", "fsdp", "tp"),
            P("fsdp", "tp"),
            P("fsdp", "tp"),
            P("outer", "fsdp", "tp"),
            P("outer", "fsdp", "tp"),
            P("outer", "fsdp", "tp"),
        ),
        out_specs=(
            P("fsdp", "tp"),
            P("fsdp", "tp"),
            P("outer", "fsdp", "tp"),
            P("outer", "fsdp", "tp"),
            P("outer", "fsdp", "tp"),
        ),
        check_vma=False,
    )
```

```python
import jax
import jax.numpy as jnp
from jax import lax
from jax.experimental import pallas as pl
from jax.experimental.pallas import tpu as pltpu
from jax.sharding import PartitionSpec as P

outer_beta = 0.9
outer_rate = 0.7
MESH = pl.DeviceIdType.MESH
BF = jnp.bfloat16
F32 = jnp.float32

Z = 8
Y = 4
PIECES = 16
STEPS = 7
SMALL = 128


def nesterov(average, params_old, moment_old):
    moment_new = outer_beta * moment_old + average
    params_new = params_old - outer_rate * (average + outer_beta * moment_new)
    return (params_new, moment_new)


def kernel(
    pg_in, par_in, mom_in, hid_in, w_in, cot_in,
    par_out, mom_out, kv_out, ig_out, wg_out,
    hid, wfull, cot, cot_t, part, sib, far, rs_out, rs_in, rs_own, kv_acc,
    pg, par, mom, y_out, y_in, pod_out, pod_in, avg,
    load_sem,
    ag_send, ag_recv, rs_send, rs_recv,
    hx_send, hx_recv, hs_send, hs_recv,
    p_send, p_recv, s_send, s_recv,
    y_send, y_recv, v_send, v_recv, pod_send, pod_recv, here_sem,
):
    o = lax.axis_index("outer")
    z = lax.axis_index("fsdp")
    t = lax.axis_index("tp")
    x = t // 2
    c = lax.rem(t, 2)
    sibling = 2 * x + (1 - c)
    peer = 2 * (1 - x) + c
    diagonal = 3 - t
    up = lax.rem(z + 1, Z)
    down = lax.rem(z + Z - 1, Z)
    y = o // 2
    x_hi = lax.rem(o, 2)
    other_hi = 2 * y + 1 - x_hi
    y_at = [lax.rem(y + i, Y) for i in range(Y)]
    half = w_in.shape[0] // 2
    quarter = pg_in.shape[1] // Y

    def remote(src, dst, send, recv, where):
        return pltpu.make_async_remote_copy(
            src_ref=src, dst_ref=dst, send_sem=send, recv_sem=recv, device_id=where, device_id_type=MESH
        )

    barrier = pltpu.get_barrier_semaphore()
    partners = [{"fsdp": up}, {"fsdp": down}, {"tp": sibling}, {"tp": peer}]
    for where in partners:
        pl.semaphore_signal(barrier, inc=1, device_id=where, device_id_type=MESH)
    pods = [other_hi] + [2 * y_at[i] + x_hi for i in range(1, Y)]
    lower = 0
    for pod in pods:
        lower += (pod < o).astype(jnp.int32)

        @pl.when(pod > o)
        def _():
            pl.semaphore_signal(barrier, inc=1, device_id={"outer": pod}, device_id_type=MESH)

    pl.semaphore_wait(barrier, len(partners) + lower)

    def ring(block):
        return lax.rem(block + 2 * Z, Z)

    def ag_piece(j, direction, at):
        if direction == 0:
            return 2 * ring(at - j // 2) + lax.rem(j, 2)
        return 2 * ring(at + j // 2) + 1 - lax.rem(j, 2)

    def ag_copy(j, direction):
        b = ag_piece(j, direction, z)
        return remote(
            wfull.at[b], wfull.at[b], ag_send.at[direction, j], ag_recv.at[direction, j],
            {"fsdp": up if direction == 0 else down},
        )

    def ag_last(part_at):
        rows = pl.ds(part_at * (half - SMALL), SMALL if part_at else half - SMALL)
        b = ag_piece(STEPS - 1, 0, z)
        return remote(
            wfull.at[b, rows], wfull.at[b, rows], ag_send.at[0, STEPS - 1 + part_at], ag_recv.at[0, STEPS - 1 + part_at],
            {"fsdp": up},
        )

    def ag_detour():
        b = ag_piece(STEPS - 2, 1, z + 1)
        rows = pl.ds(half - SMALL, SMALL)
        return remote(
            wfull.at[b, rows], wfull.at[b, rows], ag_send.at[1, STEPS], ag_recv.at[0, STEPS], {"fsdp": down}
        )

    def ag_first(j, direction):
        h = j if direction == 0 else 1 - j
        return remote(
            w_in.at[pl.ds(h * half, half)], wfull.at[2 * z + h], ag_send.at[direction, j], ag_recv.at[direction, j],
            {"fsdp": up if direction == 0 else down},
        )

    for j in range(2):
        for direction in range(2):
            ag_first(j, direction).start()

    def farther(of):
        low = ring(2 * of - z)
        high = ring(2 * of + 1 - z)
        return (jnp.minimum(high, Z - high) > jnp.minimum(low, Z - low)).astype(jnp.int32)

    def hid_turn(i, of):
        first = farther(of)
        return 2 * lax.rem(first + i // 2, 2) + i % 2

    def hid_view(k):
        return hid_in.at[:, pl.ds(pl.multiple_of(k * half, half), half)]

    def hx_copy(i):
        k = hid_turn(i, t)
        return remote(hid_view(k), hid.at[4 * t + k], hx_send.at[i], hx_recv.at[i], {"tp": peer})

    def hs_copy(k):
        b = 4 * t + k
        return remote(hid_view(k), hid.at[b], hs_send.at[k], hs_recv.at[b], {"tp": sibling})

    def hf_copy(i):
        b = 4 * peer + hid_turn(i, peer)
        return remote(hid.at[b], hid.at[b], hs_send.at[4 + i], hs_recv.at[b], {"tp": sibling})

    for i in range(4):
        hx_copy(i).start()
    loads = [pltpu.make_async_copy(cot_in, cot, load_sem.at[0])]
    for h in range(2):
        loads.append(pltpu.make_async_copy(w_in.at[pl.ds(h * half, half)], wfull.at[2 * z + h], load_sem.at[1 + h]))
    for k in range(4):
        loads.append(pltpu.make_async_copy(hid_view(k), hid.at[4 * t + k], load_sem.at[3 + k]))
    loads.append(pltpu.make_async_copy(pg_in, pg, load_sem.at[7]))
    loads.append(pltpu.make_async_copy(par_in, par, load_sem.at[8]))
    loads.append(pltpu.make_async_copy(mom_in, mom, load_sem.at[9]))
    for copy in loads:
        copy.start()
    for k in range(4):
        hs_copy(k).start()
    for copy in loads:
        copy.wait()
    cot_t[...] = cot[...].astype(F32).T.astype(BF)

    def y_copy(i):
        return remote(y_out.at[i], y_in.at[i], y_send.at[i], y_recv.at[i], {"outer": 2 * y_at[i] + x_hi})

    def pod_copy():
        return remote(pod_out, pod_in, pod_send, pod_recv, {"outer": other_hi})

    def v_copy(i):
        return remote(avg.at[y], avg.at[y], v_send.at[i], v_recv.at[i], {"outer": 2 * y_at[i] + x_hi})

    def pg_quarter(at):
        return pg[:, pl.ds(pl.multiple_of(at * quarter, quarter), quarter)].astype(BF)

    for pod in pods:
        @pl.when(pod < o)
        def _():
            pl.semaphore_signal(here_sem, inc=1, device_id={"outer": pod}, device_id_type=MESH)

    def column_part(b):
        part[b] = lax.dot_general(
            cot[...], wfull[b], (((1,), (1,)), ((), ())), preferred_element_type=F32
        ).astype(BF)

    def slot_of(b):
        return 4 * (b // 8) + lax.rem(b, 4)

    def owner_core(b):
        return lax.rem(b // 4, 2)

    def p_copy(b):
        s = slot_of(b)
        return remote(part.at[b], sib.at[s], p_send.at[s], p_recv.at[s], {"tp": sibling})

    def s_copy(b):
        k = lax.rem(b, 4)
        return remote(part.at[b], far.at[k], s_send.at[k], s_recv.at[k], {"tp": peer})

    def make_part(b):
        column_part(b)

        @pl.when(owner_core(b) != c)
        def _():
            p_copy(b).start()

    def pair_part(b):
        @pl.when((owner_core(b) == c) & (b // 8 != x))
        def _():
            p_copy(b).wait_recv()
            part[b] = (part[b].astype(F32) + sib[slot_of(b)].astype(F32)).astype(BF)
            s_copy(b).start()

    def pair_step(j, carry):
        pair_part(ag_piece(j, 0, z - 1))
        pair_part(ag_piece(j, 1, z + 1))
        return carry

    def rs_piece(j, direction):
        if direction == 0:
            return 2 * ring(z + 4 - (j + 1) // 2) + lax.rem(j, 2)
        return 2 * ring(z - 4 + (j + 1) // 2) + 1 - lax.rem(j, 2)

    def rs_copy(j, direction):
        return remote(
            rs_out.at[direction, j], rs_in.at[direction, j], rs_send.at[direction, j], rs_recv.at[direction, j],
            {"fsdp": up if direction == 0 else down},
        )

    def token_sum(b):
        @pl.when(owner_core(b) != c)
        def _():
            remote(hid.at[b], hid.at[b], hs_send.at[0], hs_recv.at[b], {"tp": sibling}).wait_recv()

        return jnp.dot(cot_t[...], hid[b], preferred_element_type=F32).T

    def rs_start(j):
        for direction in range(2):
            rs_out[direction, j] = token_sum(rs_piece(j, direction)).astype(BF)
            rs_copy(j, direction).start()

    make_part(2 * z)
    make_part(2 * z + 1)

    def ag_step(j, carry):
        @pl.when(j < STEPS - 1)
        def _():
            ag_copy(j, 0).wait_recv()

        @pl.when(j == STEPS - 1)
        def _():
            ag_last(0).wait_recv()
            ag_last(1).wait_recv()

        @pl.when(j + 2 < STEPS - 1)
        def _():
            ag_copy(j + 2, 0).start()

        @pl.when(j + 2 == STEPS - 1)
        def _():
            ag_last(0).start()

            @pl.when(z != Z - 1)
            def _():
                ag_last(1).start()

        ag_copy(j, 1).wait_recv()

        @pl.when(j + 2 < STEPS)
        def _():
            ag_copy(j + 2, 1).start()

        @pl.when((j == STEPS - 2) & (z == 1))
        def _():
            ag_detour().start()

        make_part(ag_piece(j, 0, z - 1))
        make_part(ag_piece(j, 1, z + 1))
        for at, i in ((1, 0), (3, 1), (4, 2), (6, 3)):
            @pl.when(j == at)
            def _():
                hx_copy(i).wait_recv()
                hf_copy(i).start()

        @pl.when(j == 1)
        def _():
            @pl.when(lower < len(pods))
            def _():
                pl.semaphore_wait(here_sem, len(pods) - lower)

            for i in range(1, Y):
                y_out[i] = pg_quarter(y_at[i])
                y_copy(i).start()

        @pl.when(j == 3)
        def _():
            total = pg_quarter(y).astype(F32)
            for i in range(1, Y):
                y_copy(i).wait_recv()
                total += y_in[i].astype(F32)
            pod_out[...] = total.astype(BF)
            pod_copy().start()

        @pl.when(j == 4)
        def _():
            pair_part(2 * z)
            pair_part(2 * z + 1)
            lax.fori_loop(0, 4, pair_step, 0)

        @pl.when(j == 5)
        def _():
            rs_start(0)

        @pl.when(j > 4)
        def _():
            pair_step(j - 1, 0)

        return carry

    lax.fori_loop(0, STEPS, ag_step, 0)
    rs_start(1)
    pair_step(STEPS - 1, 0)

    pod_copy().wait_recv()
    avg[y] = ((pod_out[...].astype(F32) + pod_in[...].astype(F32)) / (2 * Y)).astype(BF)
    for i in range(1, Y):
        v_copy(i).start()

    def add_keys_values(j):
        for direction in range(2):
            b = rs_piece(j, direction)
            kv_acc[...] += jnp.dot(hid[b], wfull[b], preferred_element_type=F32)

    kv_acc[...] = jnp.zeros_like(kv_acc)

    def rs_step(j, carry):
        for direction in range(2):
            mine = token_sum(rs_piece(j, direction))
            rs_copy(j - 2, direction).wait_recv()
            rs_out[direction, j] = (mine + rs_in[direction, j - 2].astype(F32)).astype(BF)
            rs_copy(j, direction).start()
        add_keys_values(j)
        return carry

    lax.fori_loop(2, STEPS - 1, rs_step, 0)

    def last_copy(part_at, direction):
        rows = pl.ds(part_at * (half // 2), half // 2)
        return remote(
            rs_out.at[direction, STEPS - 1, rows], rs_in.at[direction, STEPS - 1, rows],
            rs_send.at[direction, STEPS - 1 + part_at], rs_recv.at[direction, STEPS - 1 + part_at],
            {"fsdp": up if direction == 0 else down},
        )

    mine = [token_sum(rs_piece(STEPS - 1, direction)) for direction in range(2)]
    for direction in range(2):
        rs_copy(STEPS - 3, direction).wait_recv()
        for part_at in range(2):
            low, high = part_at * (half // 2), (part_at + 1) * (half // 2)
            total = mine[direction][low:high] + rs_in[direction, STEPS - 3, low:high].astype(F32)
            rs_out[direction, STEPS - 1, low:high] = total.astype(BF)
            last_copy(part_at, direction).start()
    add_keys_values(STEPS - 1)
    for h in range(2):
        rs_own[h] = token_sum(2 * z + h)
    for j in range(2):
        add_keys_values(j)
    for h in range(2):
        kv_acc[...] += jnp.dot(hid[2 * z + h], wfull[2 * z + h], preferred_element_type=F32)
    kv_out[...] = kv_acc[...].astype(BF)

    for i in range(1, Y):
        v_copy(i).wait_recv()
    for i in range(Y):
        columns = pl.ds(i * quarter, quarter)
        average = avg[i].astype(F32)
        new_params, new_momentum = nesterov(average, par[:, columns], mom[:, columns])
        par_out[:, columns] = new_params
        mom_out[:, columns] = new_momentum

    for k in range(4):
        b = 4 * t + k
        p_copy(b).wait_recv()
        s_copy(b).wait_recv()
        total = part[b].astype(F32) + sib[4 * x + k].astype(F32) + far[k].astype(F32)
        ig_out[:, pl.ds(k * half, half)] = total.astype(BF)

    ag_last(0).wait_send()

    @pl.when(z != Z - 1)
    def _():
        ag_last(1).wait_send()

    @pl.when(z == 1)
    def _():
        ag_detour().wait_send()

    for j in range(STEPS):
        for direction in range(2):
            if j < STEPS - 1 or direction == 1:
                ag_copy(j, direction).wait_send()
            if j < STEPS - 2:
                rs_copy(j, direction).wait_send()
    for k in range(4):
        hx_copy(k).wait_send()
        hs_copy(k).wait_send()
        hf_copy(k).wait_send()
        s_copy(4 * peer + k).wait_send()
        p_copy(4 * sibling + k).wait_send()
        p_copy(4 * diagonal + k).wait_send()
    for i in range(1, Y):
        y_copy(i).wait_send()
        v_copy(i).wait_send()
    pod_copy().wait_send()

    for direction in range(2):
        rs_copy(STEPS - 2, direction).wait_recv()
        rs_own[1 - direction] += rs_in[direction, STEPS - 2].astype(F32)
    for part_at in range(2):
        for direction in range(2):
            last_copy(part_at, direction).wait_recv()
            low, high = part_at * (half // 2), (part_at + 1) * (half // 2)
            total = rs_own[direction, low:high] + rs_in[direction, STEPS - 1, low:high].astype(F32)
            wg_out[direction * half + low:direction * half + high] = total.astype(BF)
    for direction in range(2):
        rs_copy(STEPS - 2, direction).wait_send()
        for part_at in range(2):
            last_copy(part_at, direction).wait_send()


def whole_step(pseudo_grad, params, momentum, hidden, weights, cotangent):
    tokens, width = hidden.shape
    rows, cols = weights.shape
    slab = params.shape
    half = rows // 2
    quarter = (slab[0], slab[1] // Y)
    sems = pltpu.SemaphoreType.DMA
    any_spec = pl.BlockSpec(memory_space=pl.ANY)
    return pl.pallas_call(
        kernel,
        out_shape=(
            pltpu.VMEM(slab, F32),
            pltpu.VMEM(slab, F32),
            pltpu.VMEM((tokens, cols), BF),
            pltpu.VMEM((tokens, width), BF),
            pltpu.VMEM((rows, cols), BF),
        ),
        in_specs=[any_spec] * 6,
        out_specs=[pl.BlockSpec(memory_space=pltpu.VMEM)] * 5,
        scratch_shapes=[
            pltpu.VMEM((PIECES, tokens, half), BF),
            pltpu.VMEM((PIECES, half, cols), BF),
            pltpu.VMEM((tokens, cols), BF),
            pltpu.VMEM((cols, tokens), BF),
            pltpu.VMEM((PIECES, tokens, half), BF),
            pltpu.VMEM((8, tokens, half), BF),
            pltpu.VMEM((4, tokens, half), BF),
            pltpu.VMEM((2, STEPS, half, cols), BF),
            pltpu.VMEM((2, STEPS, half, cols), BF),
            pltpu.VMEM((2, half, cols), F32),
            pltpu.VMEM((tokens, cols), F32),
            pltpu.VMEM(slab, F32),
            pltpu.VMEM(slab, F32),
            pltpu.VMEM(slab, F32),
            pltpu.VMEM((Y,) + quarter, BF),
            pltpu.VMEM((Y,) + quarter, BF),
            pltpu.VMEM(quarter, BF),
            pltpu.VMEM(quarter, BF),
            pltpu.VMEM((Y,) + quarter, BF),
            sems((10,)),
            sems((2, STEPS + 1)), sems((2, STEPS + 1)), sems((2, STEPS + 1)), sems((2, STEPS + 1)),
            sems((4,)), sems((4,)), sems((8,)), sems((PIECES,)),
            sems((8,)), sems((8,)), sems((4,)), sems((4,)),
            sems((Y,)), sems((Y,)), sems((Y,)), sems((Y,)), sems, sems, pltpu.SemaphoreType.REGULAR,
        ],
        compiler_params=pltpu.CompilerParams(
            collective_id=0, has_side_effects=True, vmem_limit_bytes=56 * 1024 * 1024
        ),
        cost_estimate=pl.CostEstimate(flops=7_250_000_000, bytes_accessed=12_000_000, transcendentals=0),
        name="whole_step",
    )(pseudo_grad, params, momentum, hidden, weights, cotangent)


def store_kernel(*refs):
    sems = refs[-1]
    count = (len(refs) - 1) // 2
    copies = [pltpu.make_async_copy(refs[i], refs[count + i], sems.at[i]) for i in range(count)]
    for copy in copies:
        copy.start()
    for copy in copies:
        copy.wait()


def store(*results):
    any_spec = pl.BlockSpec(memory_space=pl.ANY)
    return pl.pallas_call(
        store_kernel,
        out_shape=tuple(pltpu.HBM(r.shape, r.dtype) for r in results),
        in_specs=[pl.BlockSpec(memory_space=pltpu.VMEM)] * len(results),
        out_specs=[pl.BlockSpec(memory_space=pltpu.HBM)] * len(results),
        scratch_shapes=[pltpu.SemaphoreType.DMA((len(results),))],
        compiler_params=pltpu.CompilerParams(vmem_limit_bytes=1024 * 1024),
        name="store_results",
    )(*results)


def per_device(pseudo_grad, outer_params, momentum, hidden, kv_weight, kv_cotangent):
    new_params, new_momentum, keys_values, input_grad, weight_grad = store(
        *(
            pltpu.with_memory_space_constraint(r, pltpu.VMEM)
            for r in whole_step(pseudo_grad[0], outer_params, momentum, hidden[0], kv_weight[0], kv_cotangent[0])
        )
    )
    return (new_params, new_momentum, keys_values[None], input_grad[None], weight_grad[None])


def solution(mesh):
    return jax.shard_map(
        per_device,
        mesh=mesh,
        in_specs=(
            P("outer", "fsdp", "tp"),
            P("fsdp", "tp"),
            P("fsdp", "tp"),
            P("outer", "fsdp", "tp"),
            P("outer", "fsdp", "tp"),
            P("outer", "fsdp", "tp"),
        ),
        out_specs=(
            P("fsdp", "tp"),
            P("fsdp", "tp"),
            P("outer", "fsdp", "tp"),
            P("outer", "fsdp", "tp"),
            P("outer", "fsdp", "tp"),
        ),
        check_vma=False,
    )
```

```python
import jax
import jax.numpy as jnp
from jax import lax
from jax.experimental import pallas as pl
from jax.experimental.pallas import tpu as pltpu
from jax.sharding import PartitionSpec as P

outer_beta = 0.9
outer_rate = 0.7
MESH = pl.DeviceIdType.MESH
BF = jnp.bfloat16
F32 = jnp.float32

Z = 8
Y = 4
PIECES = 16
STEPS = 7
SMALL = 128


def nesterov(average, params_old, moment_old):
    moment_new = outer_beta * moment_old + average
    params_new = params_old - outer_rate * (average + outer_beta * moment_new)
    return (params_new, moment_new)


def kernel(
    pg_in, par_in, mom_in, hid_in, w_in, cot_in,
    par_out, mom_out, kv_out, ig_out, wg_out,
    hid, wfull, cot, cot_t, part, sib, far, rs_out, rs_in, rs_own, kv_acc,
    pg, par, mom, y_out, y_in, pod_out, pod_in, avg,
    load_sem,
    ag_send, ag_recv, rs_send, rs_recv,
    hx_send, hx_recv, hs_send, hs_recv,
    p_send, p_recv, s_send, s_recv,
    y_send, y_recv, v_send, v_recv, pod_send, pod_recv, here_sem,
):
    o = lax.axis_index("outer")
    z = lax.axis_index("fsdp")
    t = lax.axis_index("tp")
    x = t // 2
    c = lax.rem(t, 2)
    sibling = 2 * x + (1 - c)
    peer = 2 * (1 - x) + c
    diagonal = 3 - t
    up = lax.rem(z + 1, Z)
    down = lax.rem(z + Z - 1, Z)
    y = o // 2
    x_hi = lax.rem(o, 2)
    other_hi = 2 * y + 1 - x_hi
    y_at = [lax.rem(y + i, Y) for i in range(Y)]
    half = w_in.shape[0] // 2
    quarter = pg_in.shape[1] // Y

    def remote(src, dst, send, recv, where):
        return pltpu.make_async_remote_copy(
            src_ref=src, dst_ref=dst, send_sem=send, recv_sem=recv, device_id=where, device_id_type=MESH
        )

    barrier = pltpu.get_barrier_semaphore()
    partners = [{"fsdp": up}, {"fsdp": down}, {"tp": sibling}, {"tp": peer}]
    for where in partners:
        pl.semaphore_signal(barrier, inc=1, device_id=where, device_id_type=MESH)
    pods = [other_hi] + [2 * y_at[i] + x_hi for i in range(1, Y)]
    lower = 0
    for pod in pods:
        lower += (pod < o).astype(jnp.int32)

        @pl.when(pod > o)
        def _():
            pl.semaphore_signal(barrier, inc=1, device_id={"outer": pod}, device_id_type=MESH)

    def hid_view(k):
        return hid_in.at[:, pl.ds(pl.multiple_of(k * half, half), half)]

    loads = [pltpu.make_async_copy(cot_in, cot, load_sem.at[0])]
    for h in range(2):
        loads.append(pltpu.make_async_copy(w_in.at[pl.ds(h * half, half)], wfull.at[2 * z + h], load_sem.at[1 + h]))
    for k in range(4):
        loads.append(pltpu.make_async_copy(hid_view(k), hid.at[4 * t + k], load_sem.at[3 + k]))
    loads.append(pltpu.make_async_copy(pg_in, pg, load_sem.at[7]))
    loads.append(pltpu.make_async_copy(par_in, par, load_sem.at[8]))
    loads.append(pltpu.make_async_copy(mom_in, mom, load_sem.at[9]))
    for copy in loads:
        copy.start()

    pl.semaphore_wait(barrier, len(partners) + lower)

    def ring(block):
        return lax.rem(block + 2 * Z, Z)

    def ag_piece(j, direction, at):
        if direction == 0:
            return 2 * ring(at - j // 2) + lax.rem(j, 2)
        return 2 * ring(at + j // 2) + 1 - lax.rem(j, 2)

    def ag_copy(j, direction):
        b = ag_piece(j, direction, z)
        return remote(
            wfull.at[b], wfull.at[b], ag_send.at[direction, j], ag_recv.at[direction, j],
            {"fsdp": up if direction == 0 else down},
        )

    def ag_last(part_at):
        rows = pl.ds(part_at * (half - SMALL), SMALL if part_at else half - SMALL)
        b = ag_piece(STEPS - 1, 0, z)
        return remote(
            wfull.at[b, rows], wfull.at[b, rows], ag_send.at[0, STEPS - 1 + part_at], ag_recv.at[0, STEPS - 1 + part_at],
            {"fsdp": up},
        )

    def ag_detour():
        b = ag_piece(STEPS - 2, 1, z + 1)
        rows = pl.ds(half - SMALL, SMALL)
        return remote(
            wfull.at[b, rows], wfull.at[b, rows], ag_send.at[1, STEPS], ag_recv.at[0, STEPS], {"fsdp": down}
        )

    def ag_first(j, direction):
        h = j if direction == 0 else 1 - j
        return remote(
            w_in.at[pl.ds(h * half, half)], wfull.at[2 * z + h], ag_send.at[direction, j], ag_recv.at[direction, j],
            {"fsdp": up if direction == 0 else down},
        )

    for j in range(2):
        for direction in range(2):
            ag_first(j, direction).start()

    def farther(of):
        low = ring(2 * of - z)
        high = ring(2 * of + 1 - z)
        return (jnp.minimum(high, Z - high) > jnp.minimum(low, Z - low)).astype(jnp.int32)

    def hid_turn(i, of):
        first = farther(of)
        return 2 * lax.rem(first + i // 2, 2) + i % 2

    def hx_copy(i):
        k = hid_turn(i, t)
        return remote(hid_view(k), hid.at[4 * t + k], hx_send.at[i], hx_recv.at[i], {"tp": peer})

    def hs_copy(k):
        b = 4 * t + k
        return remote(hid_view(k), hid.at[b], hs_send.at[k], hs_recv.at[b], {"tp": sibling})

    def hf_copy(i):
        b = 4 * peer + hid_turn(i, peer)
        return remote(hid.at[b], hid.at[b], hs_send.at[4 + i], hs_recv.at[b], {"tp": sibling})

    for i in range(4):
        hx_copy(i).start()
    for k in range(4):
        hs_copy(k).start()
    for copy in loads:
        copy.wait()
    cot_t[...] = cot[...].astype(F32).T.astype(BF)

    def y_copy(i):
        return remote(y_out.at[i], y_in.at[i], y_send.at[i], y_recv.at[i], {"outer": 2 * y_at[i] + x_hi})

    def pod_copy():
        return remote(pod_out, pod_in, pod_send, pod_recv, {"outer": other_hi})

    def v_copy(i):
        return remote(avg.at[y], avg.at[y], v_send.at[i], v_recv.at[i], {"outer": 2 * y_at[i] + x_hi})

    def pg_quarter(at):
        return pg[:, pl.ds(pl.multiple_of(at * quarter, quarter), quarter)].astype(BF)

    for pod in pods:
        @pl.when(pod < o)
        def _():
            pl.semaphore_signal(here_sem, inc=1, device_id={"outer": pod}, device_id_type=MESH)

    def column_part(b):
        part[b] = lax.dot_general(
            cot[...], wfull[b], (((1,), (1,)), ((), ())), preferred_element_type=F32
        ).astype(BF)

    def slot_of(b):
        return 4 * (b // 8) + lax.rem(b, 4)

    def owner_core(b):
        return lax.rem(b // 4, 2)

    def p_copy(b):
        s = slot_of(b)
        return remote(part.at[b], sib.at[s], p_send.at[s], p_recv.at[s], {"tp": sibling})

    def s_copy(b):
        k = lax.rem(b, 4)
        return remote(part.at[b], far.at[k], s_send.at[k], s_recv.at[k], {"tp": peer})

    def make_part(b):
        column_part(b)

        @pl.when(owner_core(b) != c)
        def _():
            p_copy(b).start()

    def pair_part(b):
        @pl.when((owner_core(b) == c) & (b // 8 != x))
        def _():
            p_copy(b).wait_recv()
            part[b] = (part[b].astype(F32) + sib[slot_of(b)].astype(F32)).astype(BF)
            s_copy(b).start()

    def pair_step(j, carry):
        pair_part(ag_piece(j, 0, z - 1))
        pair_part(ag_piece(j, 1, z + 1))
        return carry

    def rs_piece(j, direction):
        if direction == 0:
            return 2 * ring(z + 4 - (j + 1) // 2) + lax.rem(j, 2)
        return 2 * ring(z - 4 + (j + 1) // 2) + 1 - lax.rem(j, 2)

    def rs_copy(j, direction):
        return remote(
            rs_out.at[direction, j], rs_in.at[direction, j], rs_send.at[direction, j], rs_recv.at[direction, j],
            {"fsdp": up if direction == 0 else down},
        )

    def token_sum(b):
        @pl.when(owner_core(b) != c)
        def _():
            remote(hid.at[b], hid.at[b], hs_send.at[0], hs_recv.at[b], {"tp": sibling}).wait_recv()

        return jnp.dot(cot_t[...], hid[b], preferred_element_type=F32).T

    def rs_start(j):
        for direction in range(2):
            rs_out[direction, j] = token_sum(rs_piece(j, direction)).astype(BF)
            rs_copy(j, direction).start()

    make_part(2 * z)
    make_part(2 * z + 1)

    def ag_step(j, carry):
        @pl.when(j < STEPS - 1)
        def _():
            ag_copy(j, 0).wait_recv()

        @pl.when(j == STEPS - 1)
        def _():
            ag_last(0).wait_recv()
            ag_last(1).wait_recv()

        @pl.when(j + 2 < STEPS - 1)
        def _():
            ag_copy(j + 2, 0).start()

        @pl.when(j + 2 == STEPS - 1)
        def _():
            ag_last(0).start()

            @pl.when(z != Z - 1)
            def _():
                ag_last(1).start()

        ag_copy(j, 1).wait_recv()

        @pl.when(j + 2 < STEPS)
        def _():
            ag_copy(j + 2, 1).start()

        @pl.when((j == STEPS - 2) & (z == 1))
        def _():
            ag_detour().start()

        make_part(ag_piece(j, 0, z - 1))
        make_part(ag_piece(j, 1, z + 1))
        for at, i in ((1, 0), (3, 1), (4, 2), (6, 3)):
            @pl.when(j == at)
            def _():
                hx_copy(i).wait_recv()
                hf_copy(i).start()

        @pl.when(j == 1)
        def _():
            @pl.when(lower < len(pods))
            def _():
                pl.semaphore_wait(here_sem, len(pods) - lower)

            for i in range(1, Y):
                y_out[i] = pg_quarter(y_at[i])
                y_copy(i).start()

        @pl.when(j == 3)
        def _():
            total = pg_quarter(y).astype(F32)
            for i in range(1, Y):
                y_copy(i).wait_recv()
                total += y_in[i].astype(F32)
            pod_out[...] = total.astype(BF)
            pod_copy().start()

        @pl.when(j == 4)
        def _():
            pair_part(2 * z)
            pair_part(2 * z + 1)
            lax.fori_loop(0, 4, pair_step, 0)

        @pl.when(j == 5)
        def _():
            rs_start(0)

        @pl.when(j > 4)
        def _():
            pair_step(j - 1, 0)

        return carry

    lax.fori_loop(0, STEPS, ag_step, 0)
    rs_start(1)
    pair_step(STEPS - 1, 0)

    pod_copy().wait_recv()
    avg[y] = ((pod_out[...].astype(F32) + pod_in[...].astype(F32)) / (2 * Y)).astype(BF)
    for i in range(1, Y):
        v_copy(i).start()

    def add_keys_values(j):
        for direction in range(2):
            b = rs_piece(j, direction)
            kv_acc[...] += jnp.dot(hid[b], wfull[b], preferred_element_type=F32)

    kv_acc[...] = jnp.zeros_like(kv_acc)

    def rs_step(j, carry):
        for direction in range(2):
            mine = token_sum(rs_piece(j, direction))
            rs_copy(j - 2, direction).wait_recv()
            rs_out[direction, j] = (mine + rs_in[direction, j - 2].astype(F32)).astype(BF)
            rs_copy(j, direction).start()
        add_keys_values(j)
        return carry

    lax.fori_loop(2, STEPS - 1, rs_step, 0)

    def last_copy(part_at, direction):
        rows = pl.ds(part_at * (half // 2), half // 2)
        return remote(
            rs_out.at[direction, STEPS - 1, rows], rs_in.at[direction, STEPS - 1, rows],
            rs_send.at[direction, STEPS - 1 + part_at], rs_recv.at[direction, STEPS - 1 + part_at],
            {"fsdp": up if direction == 0 else down},
        )

    mine = [token_sum(rs_piece(STEPS - 1, direction)) for direction in range(2)]
    for direction in range(2):
        rs_copy(STEPS - 3, direction).wait_recv()
        for part_at in range(2):
            low, high = part_at * (half // 2), (part_at + 1) * (half // 2)
            total = mine[direction][low:high] + rs_in[direction, STEPS - 3, low:high].astype(F32)
            rs_out[direction, STEPS - 1, low:high] = total.astype(BF)
            last_copy(part_at, direction).start()
    add_keys_values(STEPS - 1)
    for h in range(2):
        rs_own[h] = token_sum(2 * z + h)
    for j in range(2):
        add_keys_values(j)
    for h in range(2):
        kv_acc[...] += jnp.dot(hid[2 * z + h], wfull[2 * z + h], preferred_element_type=F32)
    kv_out[...] = kv_acc[...].astype(BF)

    for i in range(1, Y):
        v_copy(i).wait_recv()
    for i in range(Y):
        columns = pl.ds(i * quarter, quarter)
        average = avg[i].astype(F32)
        new_params, new_momentum = nesterov(average, par[:, columns], mom[:, columns])
        par_out[:, columns] = new_params
        mom_out[:, columns] = new_momentum

    for k in range(4):
        b = 4 * t + k
        p_copy(b).wait_recv()
        s_copy(b).wait_recv()
        total = part[b].astype(F32) + sib[4 * x + k].astype(F32) + far[k].astype(F32)
        ig_out[:, pl.ds(k * half, half)] = total.astype(BF)

    ag_last(0).wait_send()

    @pl.when(z != Z - 1)
    def _():
        ag_last(1).wait_send()

    @pl.when(z == 1)
    def _():
        ag_detour().wait_send()

    for j in range(STEPS):
        for direction in range(2):
            if j < STEPS - 1 or direction == 1:
                ag_copy(j, direction).wait_send()
            if j < STEPS - 2:
                rs_copy(j, direction).wait_send()
    for k in range(4):
        hx_copy(k).wait_send()
        hs_copy(k).wait_send()
        hf_copy(k).wait_send()
        s_copy(4 * peer + k).wait_send()
        p_copy(4 * sibling + k).wait_send()
        p_copy(4 * diagonal + k).wait_send()
    for i in range(1, Y):
        y_copy(i).wait_send()
        v_copy(i).wait_send()
    pod_copy().wait_send()

    for direction in range(2):
        rs_copy(STEPS - 2, direction).wait_recv()
        rs_own[1 - direction] += rs_in[direction, STEPS - 2].astype(F32)
    for part_at in range(2):
        for direction in range(2):
            last_copy(part_at, direction).wait_recv()
            low, high = part_at * (half // 2), (part_at + 1) * (half // 2)
            total = rs_own[direction, low:high] + rs_in[direction, STEPS - 1, low:high].astype(F32)
            wg_out[direction * half + low:direction * half + high] = total.astype(BF)
    for direction in range(2):
        rs_copy(STEPS - 2, direction).wait_send()
        for part_at in range(2):
            last_copy(part_at, direction).wait_send()


def whole_step(pseudo_grad, params, momentum, hidden, weights, cotangent):
    tokens, width = hidden.shape
    rows, cols = weights.shape
    slab = params.shape
    half = rows // 2
    quarter = (slab[0], slab[1] // Y)
    sems = pltpu.SemaphoreType.DMA
    any_spec = pl.BlockSpec(memory_space=pl.ANY)
    return pl.pallas_call(
        kernel,
        out_shape=(
            pltpu.VMEM(slab, F32),
            pltpu.VMEM(slab, F32),
            pltpu.VMEM((tokens, cols), BF),
            pltpu.VMEM((tokens, width), BF),
            pltpu.VMEM((rows, cols), BF),
        ),
        in_specs=[any_spec] * 6,
        out_specs=[pl.BlockSpec(memory_space=pltpu.VMEM)] * 5,
        scratch_shapes=[
            pltpu.VMEM((PIECES, tokens, half), BF),
            pltpu.VMEM((PIECES, half, cols), BF),
            pltpu.VMEM((tokens, cols), BF),
            pltpu.VMEM((cols, tokens), BF),
            pltpu.VMEM((PIECES, tokens, half), BF),
            pltpu.VMEM((8, tokens, half), BF),
            pltpu.VMEM((4, tokens, half), BF),
            pltpu.VMEM((2, STEPS, half, cols), BF),
            pltpu.VMEM((2, STEPS, half, cols), BF),
            pltpu.VMEM((2, half, cols), F32),
            pltpu.VMEM((tokens, cols), F32),
            pltpu.VMEM(slab, F32),
            pltpu.VMEM(slab, F32),
            pltpu.VMEM(slab, F32),
            pltpu.VMEM((Y,) + quarter, BF),
            pltpu.VMEM((Y,) + quarter, BF),
            pltpu.VMEM(quarter, BF),
            pltpu.VMEM(quarter, BF),
            pltpu.VMEM((Y,) + quarter, BF),
            sems((10,)),
            sems((2, STEPS + 1)), sems((2, STEPS + 1)), sems((2, STEPS + 1)), sems((2, STEPS + 1)),
            sems((4,)), sems((4,)), sems((8,)), sems((PIECES,)),
            sems((8,)), sems((8,)), sems((4,)), sems((4,)),
            sems((Y,)), sems((Y,)), sems((Y,)), sems((Y,)), sems, sems, pltpu.SemaphoreType.REGULAR,
        ],
        compiler_params=pltpu.CompilerParams(
            collective_id=0, has_side_effects=True, vmem_limit_bytes=56 * 1024 * 1024
        ),
        cost_estimate=pl.CostEstimate(flops=7_250_000_000, bytes_accessed=12_000_000, transcendentals=0),
        name="whole_step",
    )(pseudo_grad, params, momentum, hidden, weights, cotangent)


def store_kernel(*refs):
    sems = refs[-1]
    count = (len(refs) - 1) // 2
    copies = [pltpu.make_async_copy(refs[i], refs[count + i], sems.at[i]) for i in range(count)]
    for copy in copies:
        copy.start()
    for copy in copies:
        copy.wait()


def store(*results):
    any_spec = pl.BlockSpec(memory_space=pl.ANY)
    return pl.pallas_call(
        store_kernel,
        out_shape=tuple(pltpu.HBM(r.shape, r.dtype) for r in results),
        in_specs=[pl.BlockSpec(memory_space=pltpu.VMEM)] * len(results),
        out_specs=[pl.BlockSpec(memory_space=pltpu.HBM)] * len(results),
        scratch_shapes=[pltpu.SemaphoreType.DMA((len(results),))],
        compiler_params=pltpu.CompilerParams(vmem_limit_bytes=1024 * 1024),
        name="store_results",
    )(*results)


def per_device(pseudo_grad, outer_params, momentum, hidden, kv_weight, kv_cotangent):
    new_params, new_momentum, keys_values, input_grad, weight_grad = store(
        *(
            pltpu.with_memory_space_constraint(r, pltpu.VMEM)
            for r in whole_step(pseudo_grad[0], outer_params, momentum, hidden[0], kv_weight[0], kv_cotangent[0])
        )
    )
    return (new_params, new_momentum, keys_values[None], input_grad[None], weight_grad[None])


def solution(mesh):
    return jax.shard_map(
        per_device,
        mesh=mesh,
        in_specs=(
            P("outer", "fsdp", "tp"),
            P("fsdp", "tp"),
            P("fsdp", "tp"),
            P("outer", "fsdp", "tp"),
            P("outer", "fsdp", "tp"),
            P("outer", "fsdp", "tp"),
        ),
        out_specs=(
            P("fsdp", "tp"),
            P("fsdp", "tp"),
            P("outer", "fsdp", "tp"),
            P("outer", "fsdp", "tp"),
            P("outer", "fsdp", "tp"),
        ),
        check_vma=False,
    )
```
